32 devices in a mesh: group: 2 (over x), rows: 16 (over z, y, core).
Axes of the slice: x: 2, y: 2, z: 4, core: 2. Of those that a mesh axis runs over, the one named last changes fastest.
Arguments:
- queries: bfloat16 [256, 3072], P(('group', 'rows')), parts along dimension 0, may hold values from -200 to 200
- prefix_keys: bfloat16 [2048, 1024], P(('group', 'rows')), parts along dimension 0, may hold values from -6 to 6
- prefix_values: bfloat16 [2048, 1024], P(('group', 'rows')), parts along dimension 0, may hold values from -6 to 6
- tree_keys: bfloat16 [256, 1024], P(('group', 'rows')), parts along dimension 0, may hold values from -12 to 12
- tree_values: bfloat16 [256, 1024], P(('group', 'rows')), parts along dimension 0, may hold values from -6 to 6
- parents: int32 [256], P('group'), parts along dimension 0, may hold values from 0 to 95, as said below
Outputs:
- attended: bfloat16 [256, 3072], P(('group', 'rows')), parts along dimension 0
The draws below stay inside these ranges and needn't reach their ends.
There are 2 independent parts, one for each index of `group`. The reference program is written for one: setup_inputs(seed, part) draws one part's arguments, and reference() takes and returns one part's arrays. A program takes and returns all parts, laid end to end along the dimension named above; each array names one. Nothing has to cross between parts.
Inputs may be any that keep to these rules, and one draw needn't show every extreme that they name: `parents`: the rows hold the candidate trees of many requests, in 4 levels of 32 rows in order; a row of the first level is a tree's root and its own parent; every other row's parent is a row of the level before its own, and the first and the last row of each later level have the last row of the level before as parent.
All inputs are finite; a program needn't handle non-finite values.
Results may differ from the reference program's by a relative error of at most 0.005.
Values may be sent and summed in bfloat16 or wider, within the bound.
No kernel may reach another device: no remote copies, remote signals or barrier semaphores. Data moves between devices by JAX's collectives and lax.ppermute only.
A program may use at most 192 MiB of HBM per device.

```python
import jax
import jax.numpy as jnp
from jax import lax

QUERY_HEADS = 24
KV_HEADS = 8
HEAD_DIM = 128
TREE_DEPTH = 4
PREFIX = 1024
CANDIDATES = 128
LEVEL_ROWS = 32


def common_terms(key):
    base = jax.random.fold_in(key, 4242)
    first, second, third = jax.random.split(base, 3)
    direction = jax.random.normal(first, (KV_HEADS, HEAD_DIM), jnp.float32)
    direction = direction * jnp.sqrt(HEAD_DIM / jnp.sum(direction * direction, axis=1, keepdims=True))
    floor_level = jnp.log(jnp.float32(PREFIX))
    boost = floor_level + jax.random.uniform(second, (CANDIDATES,), jnp.float32, -2.5, 0.5)
    lift = 1.0 + 0.003 * jax.random.uniform(third, (CANDIDATES,), jnp.float32)
    return (direction, boost, lift)


def draw_queries(key, part):
    direction, boost, lift = common_terms(key)
    noise = jax.random.normal(jax.random.fold_in(key, 17), (CANDIDATES, KV_HEADS, QUERY_HEADS // KV_HEADS, HEAD_DIM), jnp.float32)
    along = (boost / jnp.sqrt(jnp.float32(HEAD_DIM)))[:, None, None, None] * direction[None, :, None, :]
    summed = jnp.clip(noise + along, -200.0, 200.0)
    return summed.reshape(CANDIDATES, QUERY_HEADS * HEAD_DIM).astype(jnp.bfloat16)


def draw_tree_keys(key, part):
    direction, boost, lift = common_terms(key)
    noise = jax.random.normal(jax.random.fold_in(key, 29), (CANDIDATES, KV_HEADS, HEAD_DIM), jnp.float32)
    inner = jnp.sum(noise * direction[None], axis=2, keepdims=True) / HEAD_DIM
    keyed = noise - inner * direction[None] + lift[:, None, None] * direction[None]
    keyed = jnp.clip(keyed, -12.0, 12.0)
    return keyed.reshape(CANDIDATES, KV_HEADS * HEAD_DIM).astype(jnp.bfloat16)


def draw_parents(key, part):
    row_ids = jnp.arange(CANDIDATES, dtype=jnp.int32)
    tier = row_ids // LEVEL_ROWS
    lowest = jnp.maximum(tier - 1, 0) * LEVEL_ROWS
    picks = jax.random.randint(jax.random.fold_in(key, 11), (CANDIDATES,), 0, LEVEL_ROWS, dtype=jnp.int32)
    chosen = lowest + picks
    within = row_ids % LEVEL_ROWS
    closing = (within == LEVEL_ROWS - 1) | (within == 0)
    chosen = jnp.where(closing, lowest + LEVEL_ROWS - 1, chosen)
    return jnp.where(tier == 0, row_ids, chosen).astype(jnp.int32)


def level_of(own_key, dims, pieces, smallest, high):
    def one(axis_at, shards_of):
        steps = jax.random.uniform(jax.random.fold_in(jax.random.fold_in(own_key, 6), axis_at), (shards_of,), jnp.float32, smallest / len(pieces), high / len(pieces))
        return jnp.repeat(jnp.exp(steps), dims[axis_at] // shards_of).reshape((-1,) + (1,) * (len(dims) - axis_at - 1))

    factor_of = one(*pieces[0])
    for cut in pieces[1:]:
        factor_of = factor_of * one(*cut)
    return factor_of


def bell_draw(own_key, extent, spread, limit, cuts=(), kind=jnp.bfloat16):
    entries = jax.random.normal(own_key, extent, jnp.float32) * spread
    if len(cuts) > 0:
        entries = level_of(own_key, extent, cuts, -0.22, 0.18) * entries
    return jnp.clip(entries, min=-limit, max=limit).astype(kind)


def setup_inputs(seed: int = 0, part: int = 0) -> dict:
    arg_keys = jax.random.split(jax.random.key(seed), 7)
    part_keys = jax.random.split(jax.random.fold_in(arg_keys[6], part), 7)
    queries = draw_queries(jax.random.fold_in(jax.random.fold_in(arg_keys[6], part), 71), part)
    prefix_keys = bell_draw(part_keys[1], (PREFIX, KV_HEADS * HEAD_DIM), 1.0, 6.0, ((0, 16),))
    prefix_values = bell_draw(part_keys[2], (PREFIX, KV_HEADS * HEAD_DIM), 1.0, 6.0, ((0, 16),))
    tree_keys = draw_tree_keys(jax.random.fold_in(jax.random.fold_in(arg_keys[6], part), 71), part)
    tree_values = bell_draw(part_keys[4], (CANDIDATES, KV_HEADS * HEAD_DIM), 1.0, 6.0, ((0, 16),))
    parents = draw_parents(jax.random.fold_in(jax.random.fold_in(arg_keys[6], part), 71), part)
    return dict(queries=queries, prefix_keys=prefix_keys, prefix_values=prefix_values, tree_keys=tree_keys, tree_values=tree_values, parents=parents)


def lineage_mask(parents, row_ids):
    walker = row_ids
    columns = jnp.arange(parents.shape[0], dtype=jnp.int32)
    allowed = walker[:, None] == columns[None, :]
    for level_step in range(TREE_DEPTH - 1):
        walker = parents[walker]
        allowed = allowed | (walker[:, None] == columns[None, :])
    return allowed


def reference(queries, prefix_keys, prefix_values, tree_keys, tree_values, parents):
    groups = QUERY_HEADS // KV_HEADS
    block = 16
    every_key = jnp.concatenate([prefix_keys, tree_keys], axis=0).astype(jnp.float32).reshape(-1, KV_HEADS, HEAD_DIM)
    every_value = jnp.concatenate([prefix_values, tree_values], axis=0).astype(jnp.float32).reshape(-1, KV_HEADS, HEAD_DIM)
    blocks = queries.reshape(CANDIDATES // block, block, KV_HEADS, groups, HEAD_DIM)
    starts = jnp.arange(CANDIDATES // block, dtype=jnp.int32) * block

    def attend(inputs):
        query_block, first_row = inputs
        row_ids = first_row + jnp.arange(block, dtype=jnp.int32)
        allowed = lineage_mask(parents, row_ids)
        visible = jnp.concatenate([jnp.ones((block, PREFIX), jnp.int32) == 1, allowed], axis=1)
        scores = jnp.einsum("rkgd,skd->rkgs", query_block.astype(jnp.float32), every_key) * HEAD_DIM ** -0.5
        scores = jnp.where(visible[:, None, None, :], scores, -jnp.inf)
        maxima = jnp.max(scores, axis=-1, keepdims=True)
        weights = jnp.exp(scores - maxima)
        masses = jnp.sum(weights, axis=-1)
        rounded = lax.optimization_barrier(weights.astype(jnp.bfloat16)).astype(jnp.float32)
        weighted = jnp.einsum("rkgs,skd->rkgd", rounded, every_value)
        result = weighted / masses[..., None]
        return result.reshape(block, QUERY_HEADS * HEAD_DIM).astype(jnp.bfloat16)

    return lax.map(attend, (blocks, starts)).reshape(CANDIDATES, QUERY_HEADS * HEAD_DIM)
```

```python
import functools

import jax
import jax.numpy as jnp
from jax import lax
from jax.experimental import pallas as pl
from jax.experimental.pallas import tpu as pltpu
from jax.sharding import PartitionSpec as P

QUERY_HEADS = 24
KV_HEADS = 8
HEAD_DIM = 128
TREE_DEPTH = 4
GROUPS = QUERY_HEADS // KV_HEADS
WIDTH = QUERY_HEADS * HEAD_DIM
LANES = 128
STRIDE = 32


def stacked(refs, columns):
    blocks = [ref[:, columns] for ref in refs]
    if blocks[0].shape[0] % 16 == 0:
        return jnp.concatenate(blocks, axis=0)
    wide = jnp.concatenate([block.astype(jnp.float32) for block in blocks], axis=0)
    return wide.astype(jnp.bfloat16)


def attend_kernel(owners, pieces, *refs):
    queries = refs[:owners]
    at = owners
    slab_keys, slab_values, tree_keys, tree_values = (
        refs[at + i * pieces : at + (i + 1) * pieces] for i in range(4)
    )
    at += 4 * pieces
    bias_ref = refs[at]
    outs = refs[at + 1 :]
    local_rows = queries[0].shape[0]
    rows = owners * local_rows
    bias = jnp.concatenate([bias_ref[...]] * GROUPS, axis=0)
    lane = lax.broadcasted_iota(jnp.int32, (rows, LANES), 1)
    stats = jnp.zeros((rows, LANES), jnp.float32)
    nt = (((1,), (1,)), ((), ()))
    for head in range(KV_HEADS):
        columns = slice(head * HEAD_DIM, (head + 1) * HEAD_DIM)
        query = jnp.concatenate(
            [
                ref[:, (head * GROUPS + g) * HEAD_DIM : (head * GROUPS + g + 1) * HEAD_DIM].astype(jnp.float32)
                for g in range(GROUPS)
                for ref in queries
            ],
            axis=0,
        ).astype(jnp.bfloat16)
        slab = lax.dot_general(query, stacked(slab_keys, columns), nt, preferred_element_type=jnp.float32)
        tree = lax.dot_general(query, stacked(tree_keys, columns), nt, preferred_element_type=jnp.float32)
        slab = slab * HEAD_DIM ** (-0.5)
        tree = tree * HEAD_DIM ** (-0.5) + bias
        maxima = jnp.maximum(
            jnp.max(slab, axis=1, keepdims=True), jnp.max(tree, axis=1, keepdims=True)
        )
        slab = jnp.exp(slab - maxima)
        tree = jnp.exp(tree - maxima)
        masses = jnp.sum(slab, axis=1, keepdims=True) + jnp.sum(tree, axis=1, keepdims=True)
        weighted = jnp.dot(
            slab.astype(jnp.bfloat16), stacked(slab_values, columns), preferred_element_type=jnp.float32
        ) + jnp.dot(
            tree.astype(jnp.bfloat16), stacked(tree_values, columns), preferred_element_type=jnp.float32
        )
        weighted = weighted / masses
        level = maxima + jnp.log(masses)
        for g in range(GROUPS):
            query_head = head * GROUPS + g
            wide = slice(query_head * HEAD_DIM, (query_head + 1) * HEAD_DIM)
            here = (lane % STRIDE == query_head) & (lane < 3 * STRIDE)
            stats = jnp.where(here, level[g * rows : (g + 1) * rows], stats)
            for owner in range(owners):
                first = g * rows + owner * local_rows
                outs[owner][:, wide] = weighted[first : first + local_rows].astype(jnp.bfloat16)
    high = stats.astype(jnp.bfloat16).astype(jnp.float32)
    rest = stats - high
    middle = rest.astype(jnp.bfloat16).astype(jnp.float32)
    low = rest - middle
    sent = jnp.where(lane < STRIDE, high, jnp.where(lane < 2 * STRIDE, middle, low))
    for owner in range(owners):
        outs[owner][:, WIDTH:] = sent[owner * local_rows : (owner + 1) * local_rows].astype(jnp.bfloat16)


def merge_kernel(*refs):
    parts, out = refs[:-1], refs[-1]
    levels = []
    for part in parts:
        terms = part[:, WIDTH:].astype(jnp.float32)
        levels.append(
            terms[:, :STRIDE] + terms[:, STRIDE : 2 * STRIDE] + terms[:, 2 * STRIDE : 3 * STRIDE]
        )
    top = functools.reduce(jnp.maximum, levels)
    shares = [jnp.exp(level - top) for level in levels]
    whole = 1.0 / functools.reduce(jnp.add, shares)
    shares = [share * whole for share in shares]
    for head in range(QUERY_HEADS):
        wide = slice(head * HEAD_DIM, (head + 1) * HEAD_DIM)
        total = functools.reduce(
            jnp.add,
            [
                share[:, head : head + 1] * part[:, wide].astype(jnp.float32)
                for share, part in zip(shares, parts)
            ],
        )
        out[:, wide] = total.astype(out.dtype)


def swap(x, offset):
    return lax.ppermute(x, "rows", [(i, i ^ offset) for i in range(lax.axis_size("rows"))])


def tree_bias(parents, row_ids, token_ids):
    columns = jnp.arange(parents.shape[0], dtype=jnp.int32)
    walker = row_ids
    allowed = walker[:, None] == token_ids[None, :]
    for _ in range(TREE_DEPTH - 1):
        walker = jnp.sum(jnp.where(walker[:, None] == columns[None, :], parents[None, :], 0), axis=1)
        allowed = allowed | (walker[:, None] == token_ids[None, :])
    return jnp.where(allowed, 0.0, -jnp.inf).astype(jnp.float32)


def shards(queries, prefix_keys, prefix_values, tree_keys, tree_values, parents):
    size = lax.axis_size("rows")
    bits = size.bit_length() - 1
    near_bits = (bits + 1) // 2
    near = 2**near_bits
    far = size // near
    local_rows = queries.shape[0]
    position = lax.axis_index("rows")

    pieces = {0: (prefix_keys, prefix_values, tree_keys, tree_values)}
    for bit in reversed(range(near_bits)):
        for offset in list(pieces):
            pieces[offset ^ (1 << bit)] = tuple(swap(x, 1 << bit) for x in pieces[offset])
    far_offsets = [near * i for i in range(far)]
    all_queries = [queries] + [swap(queries, offset) for offset in far_offsets[1:]]

    slots = jnp.arange(local_rows, dtype=jnp.int32)[None, :]
    row_ids = ((position ^ jnp.array(far_offsets, jnp.int32))[:, None] * local_rows + slots).reshape(-1)
    offsets = sorted(pieces)
    token_ids = ((position ^ jnp.array(offsets, jnp.int32))[:, None] * local_rows + slots).reshape(-1)
    bias = tree_bias(parents, row_ids, token_ids)

    operands = all_queries + [pieces[offset][i] for i in range(4) for offset in offsets] + [bias]
    vmem = pl.BlockSpec(memory_space=pltpu.VMEM)
    partials = pl.pallas_call(
        functools.partial(attend_kernel, far, near),
        out_shape=[jax.ShapeDtypeStruct((local_rows, WIDTH + LANES), jnp.bfloat16)] * far,
        in_specs=[vmem] * len(operands),
        out_specs=[vmem] * far,
        compiler_params=pltpu.CompilerParams(vmem_limit_bytes=32 * 2**20),
    )(*operands)
    parts = [partials[0]] + [swap(partials[i], far_offsets[i]) for i in range(1, far)]
    return pl.pallas_call(
        merge_kernel,
        out_shape=jax.ShapeDtypeStruct((local_rows, WIDTH), jnp.bfloat16),
        in_specs=[vmem] * far,
        out_specs=vmem,
    )(*parts)


def solution(mesh):
    placed = (
        P(("group", "rows"), None),
        P(("group", "rows"), None),
        P(("group", "rows"), None),
        P(("group", "rows"), None),
        P(("group", "rows"), None),
        P("group"),
    )
    return jax.shard_map(
        shards, mesh=mesh, in_specs=placed, out_specs=P(("group", "rows"), None), check_vma=False
    )
```

```python
import functools

import jax
import jax.numpy as jnp
from jax import lax
from jax.experimental import pallas as pl
from jax.experimental.pallas import tpu as pltpu
from jax.sharding import PartitionSpec as P

QUERY_HEADS = 24
KV_HEADS = 8
HEAD_DIM = 128
TREE_DEPTH = 4
GROUPS = QUERY_HEADS // KV_HEADS
WIDTH = QUERY_HEADS * HEAD_DIM
LANES = 128
STRIDE = 32


def prepare_kernel(
    near, queries, prefix_keys, prefix_values, tree_keys, tree_values, parents,
    own_queries, own, bias, tree_scratch, parent_scratch, sems,
):
    slab = prefix_keys.shape[0]
    copies = [
        pltpu.make_async_copy(prefix_keys, own.at[:slab], sems.at[0]),
        pltpu.make_async_copy(prefix_values, own.at[slab : 2 * slab], sems.at[1]),
        pltpu.make_async_copy(tree_keys, tree_scratch.at[0], sems.at[2]),
        pltpu.make_async_copy(tree_values, tree_scratch.at[1], sems.at[3]),
        pltpu.make_async_copy(queries, own_queries, sems.at[4]),
    ]
    parent_copy = pltpu.make_async_copy(parents, parent_scratch, sems.at[5])
    parent_copy.start()
    for copy in copies:
        copy.start()
    position = lax.axis_index("rows")
    local_rows = queries.shape[0]
    rows, tokens = bias.shape
    slot = lax.broadcasted_iota(jnp.int32, (rows, 1), 0)
    walker = (position ^ (slot // local_rows * near)) * local_rows + slot % local_rows
    slot = lax.broadcasted_iota(jnp.int32, (1, tokens), 1)
    token = (position ^ (slot // local_rows)) * local_rows + slot % local_rows
    columns = lax.broadcasted_iota(jnp.int32, (rows, parents.shape[1]), 1)
    allowed = walker == token
    parent_copy.wait()
    parent = parent_scratch[...]
    for _ in range(TREE_DEPTH - 1):
        walker = jnp.sum(jnp.where(walker == columns, parent, 0), axis=1, keepdims=True)
        allowed = allowed | (walker == token)
    bias[...] = jnp.where(allowed, 0.0, -jnp.inf)
    for copy in copies:
        copy.wait()
    both = jnp.concatenate([tree_scratch[0].astype(jnp.float32), tree_scratch[1].astype(jnp.float32)], axis=0)
    own[2 * slab :] = both.astype(own.dtype)


def attend_kernel(owners, pieces, *refs):
    queries = refs[:owners]
    blocks = refs[owners : owners + pieces]
    bias_ref = refs[owners + pieces]
    outs = refs[owners + pieces + 1 :]
    local_rows = queries[0].shape[0]
    rows = owners * local_rows
    slab_rows = (blocks[0].shape[0] - 2 * local_rows) // 2
    bias = jnp.concatenate([bias_ref[...]] * GROUPS, axis=0)
    lane = lax.broadcasted_iota(jnp.int32, (rows, LANES), 1)
    stats = jnp.zeros((rows, LANES), jnp.float32)
    nt = (((1,), (1,)), ((), ()))
    for head in range(KV_HEADS):
        columns = slice(head * HEAD_DIM, (head + 1) * HEAD_DIM)
        query = jnp.concatenate(
            [
                ref[:, (head * GROUPS + g) * HEAD_DIM : (head * GROUPS + g + 1) * HEAD_DIM].astype(jnp.float32)
                for g in range(GROUPS)
                for ref in queries
            ],
            axis=0,
        ).astype(jnp.bfloat16)
        slab_keys = jnp.concatenate([ref[:slab_rows, columns] for ref in blocks], axis=0)
        slab_values = jnp.concatenate([ref[slab_rows : 2 * slab_rows, columns] for ref in blocks], axis=0)
        trees = [ref[2 * slab_rows :, columns].astype(jnp.float32) for ref in blocks]
        tree_keys = jnp.concatenate([tree[:local_rows] for tree in trees], axis=0).astype(jnp.bfloat16)
        tree_values = jnp.concatenate([tree[local_rows:] for tree in trees], axis=0).astype(jnp.bfloat16)
        slab = lax.dot_general(query, slab_keys, nt, preferred_element_type=jnp.float32)
        tree = lax.dot_general(query, tree_keys, nt, preferred_element_type=jnp.float32)
        slab = slab * HEAD_DIM ** (-0.5)
        tree = tree * HEAD_DIM ** (-0.5) + bias
        maxima = jnp.maximum(
            jnp.max(slab, axis=1, keepdims=True), jnp.max(tree, axis=1, keepdims=True)
        )
        slab = jnp.exp(slab - maxima)
        tree = jnp.exp(tree - maxima)
        masses = jnp.sum(slab, axis=1, keepdims=True) + jnp.sum(tree, axis=1, keepdims=True)
        weighted = jnp.dot(
            slab.astype(jnp.bfloat16), slab_values, preferred_element_type=jnp.float32
        ) + jnp.dot(tree.astype(jnp.bfloat16), tree_values, preferred_element_type=jnp.float32)
        weighted = weighted / masses
        level = maxima + jnp.log(masses)
        for g in range(GROUPS):
            query_head = head * GROUPS + g
            wide = slice(query_head * HEAD_DIM, (query_head + 1) * HEAD_DIM)
            here = (lane % STRIDE == query_head) & (lane < 3 * STRIDE)
            stats = jnp.where(here, level[g * rows : (g + 1) * rows], stats)
            for owner in range(owners):
                first = g * rows + owner * local_rows
                outs[owner][:, wide] = weighted[first : first + local_rows].astype(jnp.bfloat16)
    high = stats.astype(jnp.bfloat16).astype(jnp.float32)
    rest = stats - high
    middle = rest.astype(jnp.bfloat16).astype(jnp.float32)
    low = rest - middle
    sent = jnp.where(lane < STRIDE, high, jnp.where(lane < 2 * STRIDE, middle, low))
    for owner in range(owners):
        outs[owner][:, WIDTH:] = sent[owner * local_rows : (owner + 1) * local_rows].astype(jnp.bfloat16)


def merge_kernel(*refs):
    parts, out = refs[:-1], refs[-1]
    levels = []
    for part in parts:
        terms = part[:, WIDTH:].astype(jnp.float32)
        levels.append(
            terms[:, :STRIDE] + terms[:, STRIDE : 2 * STRIDE] + terms[:, 2 * STRIDE : 3 * STRIDE]
        )
    top = functools.reduce(jnp.maximum, levels)
    shares = [jnp.exp(level - top) for level in levels]
    whole = 1.0 / functools.reduce(jnp.add, shares)
    shares = [share * whole for share in shares]
    for head in range(QUERY_HEADS):
        wide = slice(head * HEAD_DIM, (head + 1) * HEAD_DIM)
        total = functools.reduce(
            jnp.add,
            [
                share[:, head : head + 1] * part[:, wide].astype(jnp.float32)
                for share, part in zip(shares, parts)
            ],
        )
        out[:, wide] = total.astype(out.dtype)


def held(memory, arrays):
    return [pltpu.with_memory_space_constraint(x, memory) for x in arrays]


def swap(x, offset):
    return lax.ppermute(x, "rows", [(i, i ^ offset) for i in range(lax.axis_size("rows"))])


def shards(queries, prefix_keys, prefix_values, tree_keys, tree_values, parents):
    size = lax.axis_size("rows")
    bits = size.bit_length() - 1
    near_bits = (bits + 1) // 2
    near = 2**near_bits
    far = size // near
    local_rows = queries.shape[0]
    slab = prefix_keys.shape[0]
    far_offsets = [near * i for i in range(far)]
    offsets = list(range(near))
    vmem = pl.BlockSpec(memory_space=pltpu.VMEM)
    hbm = pl.BlockSpec(memory_space=pltpu.HBM)
    own_queries, own, bias = pl.pallas_call(
        functools.partial(prepare_kernel, near),
        out_shape=[
            pltpu.VMEM(queries.shape, queries.dtype),
            pltpu.VMEM((2 * (slab + local_rows), prefix_keys.shape[1]), prefix_keys.dtype),
            pltpu.VMEM((far * local_rows, near * local_rows), jnp.float32),
        ],
        in_specs=[hbm] * 6,
        out_specs=[vmem] * 3,
        scratch_shapes=[
            pltpu.VMEM((2,) + tree_keys.shape, tree_keys.dtype),
            pltpu.VMEM((1,) + parents.shape, parents.dtype),
            pltpu.SemaphoreType.DMA((6,)),
        ],
        compiler_params=pltpu.CompilerParams(vmem_limit_bytes=16 * 2**20),
    )(*held(pltpu.HBM, [queries, prefix_keys, prefix_values, tree_keys, tree_values, parents[None, :]]))

    all_queries = [own_queries] + [swap(queries, offset) for offset in far_offsets[1:]]
    pieces = {0: own}
    for bit in reversed(range(near_bits)):
        for offset in list(pieces):
            piece = pieces[offset]
            if bit == 0 and offset:
                piece, *all_queries = lax.optimization_barrier((piece, *all_queries))
            pieces[offset ^ (1 << bit)] = swap(piece, 1 << bit)

    operands = all_queries + [pieces[offset] for offset in offsets] + [bias]
    partials = pl.pallas_call(
        functools.partial(attend_kernel, far, near),
        out_shape=[pltpu.VMEM((local_rows, WIDTH + LANES), jnp.bfloat16)] * far,
        in_specs=[vmem] * len(operands),
        out_specs=[vmem] * far,
        compiler_params=pltpu.CompilerParams(vmem_limit_bytes=32 * 2**20),
    )(*held(pltpu.VMEM, operands))
    parts = [partials[0]] + [swap(partials[i], far_offsets[i]) for i in range(1, far)]
    return pl.pallas_call(
        merge_kernel,
        out_shape=jax.ShapeDtypeStruct((local_rows, WIDTH), jnp.bfloat16),
        in_specs=[vmem] * far,
        out_specs=vmem,
        compiler_params=pltpu.CompilerParams(vmem_limit_bytes=16 * 2**20),
    )(*held(pltpu.VMEM, parts))


def solution(mesh):
    placed = (
        P(("group", "rows"), None),
        P(("group", "rows"), None),
        P(("group", "rows"), None),
        P(("group", "rows"), None),
        P(("group", "rows"), None),
        P("group"),
    )
    return jax.shard_map(
        shards, mesh=mesh, in_specs=placed, out_specs=P(("group", "rows"), None), check_vma=False
    )
```

```python
import functools

import jax
import jax.numpy as jnp
from jax import lax
from jax.experimental import pallas as pl
from jax.experimental.pallas import tpu as pltpu
from jax.sharding import PartitionSpec as P

QUERY_HEADS = 24
KV_HEADS = 8
HEAD_DIM = 128
TREE_DEPTH = 4
GROUPS = QUERY_HEADS // KV_HEADS
WIDTH = QUERY_HEADS * HEAD_DIM
LANES = 128
STRIDE = 32
NT = (((1,), (1,)), ((), ()))


def prepare_kernel(
    queries, prefix_keys, prefix_values, tree_keys, tree_values,
    own_queries, own, tree_scratch, sems,
):
    slab = prefix_keys.shape[0]
    copies = [
        pltpu.make_async_copy(tree_keys, tree_scratch.at[0], sems.at[0]),
        pltpu.make_async_copy(tree_values, tree_scratch.at[1], sems.at[1]),
        pltpu.make_async_copy(prefix_keys, own.at[:slab], sems.at[2]),
        pltpu.make_async_copy(prefix_values, own.at[slab : 2 * slab], sems.at[3]),
        pltpu.make_async_copy(queries, own_queries, sems.at[4]),
    ]
    for copy in copies:
        copy.start()
    for copy in copies:
        copy.wait()
    both = jnp.concatenate(
        [tree_scratch[0].astype(jnp.float32), tree_scratch[1].astype(jnp.float32)], axis=0
    ).astype(own.dtype)
    own[2 * slab :] = both


def mask_kernel(near, local_rows, parents, bias):
    position = lax.axis_index("rows")
    rows, tokens = bias.shape
    slot = lax.broadcasted_iota(jnp.int32, (rows, 1), 0)
    walker = (position ^ (slot // local_rows * near)) * local_rows + slot % local_rows
    slot = lax.broadcasted_iota(jnp.int32, (1, tokens), 1)
    token = (position ^ (slot // local_rows)) * local_rows + slot % local_rows
    columns = lax.broadcasted_iota(jnp.int32, (rows, parents.shape[1]), 1)
    parent = parents[...]
    allowed = walker == token
    for _ in range(TREE_DEPTH - 1):
        walker = jnp.sum(jnp.where(walker == columns, parent, 0), axis=1, keepdims=True)
        allowed = allowed | (walker == token)
    bias[...] = jnp.where(allowed, 0.0, -jnp.inf)


def attend_kernel(owners, *refs):
    queries, outs = refs[:owners], refs[-owners:]
    blocks, bias_ref = refs[owners : -owners - 1], refs[-owners - 1]
    local_rows = queries[0].shape[0]
    rows = owners * local_rows
    slab = (blocks[0].shape[0] - 2 * local_rows) // 2
    key_parts = [ref.at[:slab] for ref in blocks]
    value_parts = [ref.at[slab : 2 * slab] for ref in blocks]
    tree_parts = [ref.at[2 * slab :] for ref in blocks]

    bias = jnp.concatenate([bias_ref[...]] * GROUPS, axis=0)
    every_query = jnp.concatenate([ref[...].astype(jnp.float32) for ref in queries], axis=0).astype(jnp.bfloat16)
    trees = [ref[...].astype(jnp.float32) for ref in tree_parts]
    tree_keys = jnp.concatenate([tree[:local_rows] for tree in trees], axis=0).astype(jnp.bfloat16)
    tree_values = jnp.concatenate([tree[local_rows:] for tree in trees], axis=0).astype(jnp.bfloat16)
    heads = [slice(head * HEAD_DIM, (head + 1) * HEAD_DIM) for head in range(QUERY_HEADS)]
    scores = []
    for head in range(KV_HEADS):
        query = jnp.concatenate([every_query[:, heads[head * GROUPS + g]] for g in range(GROUPS)], axis=0)
        keys = jnp.concatenate([ref[:, heads[head]] for ref in key_parts], axis=0)
        slab_scores = lax.dot_general(query, keys, NT, preferred_element_type=jnp.float32)
        tree_scores = lax.dot_general(query, tree_keys[:, heads[head]], NT, preferred_element_type=jnp.float32)
        scores.append((slab_scores * HEAD_DIM ** (-0.5), tree_scores * HEAD_DIM ** (-0.5) + bias))
    weights = []
    for slab_scores, tree_scores in scores:
        maxima = jnp.maximum(
            jnp.max(slab_scores, axis=1, keepdims=True), jnp.max(tree_scores, axis=1, keepdims=True)
        )
        slab_weights = jnp.exp(slab_scores - maxima)
        tree_weights = jnp.exp(tree_scores - maxima)
        masses = jnp.sum(slab_weights, axis=1, keepdims=True) + jnp.sum(tree_weights, axis=1, keepdims=True)
        weights.append(
            (slab_weights.astype(jnp.bfloat16), tree_weights.astype(jnp.bfloat16), masses, maxima + jnp.log(masses))
        )
    lane = lax.broadcasted_iota(jnp.int32, (rows, LANES), 1)
    stats = jnp.zeros((rows, LANES), jnp.float32)
    for head, (slab_weights, tree_weights, masses, level) in enumerate(weights):
        values = jnp.concatenate([ref[:, heads[head]] for ref in value_parts], axis=0)
        weighted = jnp.dot(slab_weights, values, preferred_element_type=jnp.float32) + jnp.dot(
            tree_weights, tree_values[:, heads[head]], preferred_element_type=jnp.float32
        )
        weighted = weighted * (1.0 / masses)
        for g in range(GROUPS):
            query_head = head * GROUPS + g
            here = (lane % STRIDE == query_head) & (lane < 3 * STRIDE)
            stats = jnp.where(here, level[g * rows : (g + 1) * rows], stats)
            for owner in range(owners):
                first = g * rows + owner * local_rows
                outs[owner][:, heads[query_head]] = weighted[first : first + local_rows].astype(jnp.bfloat16)
    high = stats.astype(jnp.bfloat16).astype(jnp.float32)
    left = stats - high
    middle = left.astype(jnp.bfloat16).astype(jnp.float32)
    low = left - middle
    sent = jnp.where(lane < STRIDE, high, jnp.where(lane < 2 * STRIDE, middle, low))
    for owner in range(owners):
        outs[owner][:, WIDTH:] = sent[owner * local_rows : (owner + 1) * local_rows].astype(jnp.bfloat16)


def merge_kernel(*refs):
    parts, out = refs[:-1], refs[-1]
    levels = []
    for part in parts:
        terms = part[:, WIDTH:].astype(jnp.float32)
        levels.append(
            terms[:, :STRIDE] + terms[:, STRIDE : 2 * STRIDE] + terms[:, 2 * STRIDE : 3 * STRIDE]
        )
    top = functools.reduce(jnp.maximum, levels)
    shares = [jnp.exp(level - top) for level in levels]
    whole = 1.0 / functools.reduce(jnp.add, shares)
    shares = [share * whole for share in shares]
    for head in range(QUERY_HEADS):
        wide = slice(head * HEAD_DIM, (head + 1) * HEAD_DIM)
        total = functools.reduce(
            jnp.add,
            [
                share[:, head : head + 1] * part[:, wide].astype(jnp.float32)
                for share, part in zip(shares, parts)
            ],
        )
        out[:, wide] = total.astype(out.dtype)


def held(memory, arrays):
    return [pltpu.with_memory_space_constraint(x, memory) for x in arrays]


def swap(x, offset):
    return lax.ppermute(x, "rows", [(i, i ^ offset) for i in range(lax.axis_size("rows"))])


def after(x, *earlier):
    return lax.optimization_barrier((x, *earlier))


def shards(queries, prefix_keys, prefix_values, tree_keys, tree_values, parents):
    size = lax.axis_size("rows")
    bits = size.bit_length() - 1
    near_bits = (bits + 1) // 2
    near = 2**near_bits
    far = size // near
    local_rows = queries.shape[0]
    slab, row_width = prefix_keys.shape
    far_offsets = [near * i for i in range(far)]
    far_order = far_offsets[-1:] + far_offsets[1:-1]
    vmem = pl.BlockSpec(memory_space=pltpu.VMEM)
    hbm = pl.BlockSpec(memory_space=pltpu.HBM)
    params = pltpu.CompilerParams(vmem_limit_bytes=16 * 2**20)
    own_queries, own = pl.pallas_call(
        prepare_kernel,
        out_shape=[
            pltpu.VMEM(queries.shape, queries.dtype),
            pltpu.VMEM((2 * (slab + local_rows), row_width), prefix_keys.dtype),
        ],
        in_specs=[hbm] * 5,
        out_specs=[vmem] * 2,
        scratch_shapes=[
            pltpu.VMEM((2,) + tree_keys.shape, tree_keys.dtype),
            pltpu.SemaphoreType.DMA((5,)),
        ],
        compiler_params=params,
    )(*held(pltpu.HBM, [queries, prefix_keys, prefix_values, tree_keys, tree_values]))
    bias = pl.pallas_call(
        functools.partial(mask_kernel, near, local_rows),
        out_shape=pltpu.VMEM((far * local_rows, near * local_rows), jnp.float32),
        in_specs=[vmem],
        out_specs=vmem,
        compiler_params=params,
    )(parents[None, :])

    all_queries = {0: own_queries}
    for offset in far_order:
        all_queries[offset] = swap(queries, offset)
    pieces = {0: own}
    for bit in reversed(range(near_bits)):
        for offset in list(pieces):
            piece = pieces[offset]
            if bit == 0 and offset:
                piece, *waited = after(piece, *all_queries.values())
                all_queries = dict(zip(all_queries, waited))
            pieces[offset ^ (1 << bit)] = swap(piece, 1 << bit)
    operands = (
        [all_queries[offset] for offset in far_offsets] + [pieces[offset] for offset in range(near)] + [bias]
    )
    partials = pl.pallas_call(
        functools.partial(attend_kernel, far),
        out_shape=[pltpu.VMEM((local_rows, WIDTH + LANES), jnp.bfloat16)] * far,
        in_specs=[vmem] * len(operands),
        out_specs=[vmem] * far,
        compiler_params=params,
    )(*held(pltpu.VMEM, operands))
    parts = [partials[0]]
    for offset in far_order:
        parts.append(swap(partials[far_offsets.index(offset)], offset))
    return pl.pallas_call(
        merge_kernel,
        out_shape=jax.ShapeDtypeStruct((local_rows, WIDTH), jnp.bfloat16),
        in_specs=[vmem] * far,
        out_specs=vmem,
        compiler_params=params,
    )(*held(pltpu.VMEM, parts))


def solution(mesh):
    placed = (
        P(("group", "rows"), None),
        P(("group", "rows"), None),
        P(("group", "rows"), None),
        P(("group", "rows"), None),
        P(("group", "rows"), None),
        P("group"),
    )
    return jax.shard_map(
        shards, mesh=mesh, in_specs=placed, out_specs=P(("group", "rows"), None), check_vma=False
    )
```

```python
import functools

import jax
import jax.numpy as jnp
from jax import lax
from jax.experimental import pallas as pl
from jax.experimental.pallas import tpu as pltpu
from jax.sharding import PartitionSpec as P

QUERY_HEADS = 24
KV_HEADS = 8
HEAD_DIM = 128
TREE_DEPTH = 4
GROUPS = QUERY_HEADS // KV_HEADS
WIDTH = QUERY_HEADS * HEAD_DIM
LANES = 128
STRIDE = 32
NT = (((1,), (1,)), ((), ()))
HEADS = [slice(head * HEAD_DIM, (head + 1) * HEAD_DIM) for head in range(QUERY_HEADS)]


def prepare_kernel(
    queries, prefix_keys, prefix_values, tree_keys, tree_values, own_queries, keys, rest, tree_scratch, sems
):
    slab = prefix_values.shape[0]
    copies = [
        pltpu.make_async_copy(tree_keys, tree_scratch.at[0], sems.at[0]),
        pltpu.make_async_copy(tree_values, tree_scratch.at[1], sems.at[1]),
        pltpu.make_async_copy(prefix_values, rest.at[:slab], sems.at[2]),
        pltpu.make_async_copy(prefix_keys, keys, sems.at[3]),
        pltpu.make_async_copy(queries, own_queries, sems.at[4]),
    ]
    for copy in copies:
        copy.start()
    for copy in copies:
        copy.wait()
    both = [tree_scratch[0].astype(jnp.float32), tree_scratch[1].astype(jnp.float32)]
    rest[slab:] = jnp.concatenate(both, axis=0).astype(rest.dtype)


def stack_kernel(*refs):
    blocks, out = refs[:-1], refs[-1]
    first = 0
    for block in blocks:
        out[first : first + block.shape[0]] = block[...]
        first += block.shape[0]


def chosen(index, values):
    picked = jnp.full(index.shape, values[0], jnp.int32)
    for place in range(1, len(values)):
        picked = jnp.where(index == place, values[place], picked)
    return picked


def mask_kernel(owner_offsets, token_offsets, local_rows, parents, bias):
    position = lax.axis_index("rows")
    rows, columns = bias.shape
    block = columns // len(token_offsets)
    slab = block - 2 * local_rows
    slot = lax.broadcasted_iota(jnp.int32, (rows, 1), 0)
    walker = (position ^ chosen(slot // local_rows, owner_offsets)) * local_rows + slot % local_rows
    slot = lax.broadcasted_iota(jnp.int32, (1, columns), 1)
    within = slot % block - slab
    token = (position ^ chosen(slot // block, token_offsets)) * local_rows + within
    is_tree = (within >= 0) & (within < local_rows)
    candidates = lax.broadcasted_iota(jnp.int32, (rows, parents.shape[1]), 1)
    parent = parents[...]
    allowed = walker == token
    for _ in range(TREE_DEPTH - 1):
        walker = jnp.sum(jnp.where(walker == candidates, parent, 0), axis=1, keepdims=True)
        allowed = allowed | (walker == token)
    bias[...] = jnp.where((allowed & is_tree) | (within < 0), 0.0, -jnp.inf)


def block_rows(parts, local_rows):
    keys, values = [], []
    for slab_keys, rest in parts:
        slab = slab_keys.shape[0]
        tree = rest[slab:]
        halves = tree.astype(jnp.float32)
        turned = jnp.concatenate([halves[local_rows:], halves[:local_rows]], axis=0)
        keys += [slab_keys[...], tree]
        values += [rest[:slab], turned.astype(jnp.bfloat16)]
    return keys, values


def bundle_parts(bundle, last_rest, count, slab, local_rows):
    block = slab + 2 * local_rows
    rests = [bundle.at[count * slab + i * block : count * slab + (i + 1) * block] for i in range(count - 1)]
    return [(bundle.at[i * slab : (i + 1) * slab], rest) for i, rest in enumerate(rests + [last_rest])]


def across(x, lanes):
    if x.shape[1] == 1:
        return x
    copies = -(-lanes // x.shape[1])
    return jnp.concatenate([x] * copies, axis=1)[:, :lanes]


def attend(queries, parts, bias, maxima_before):
    key_parts, value_parts = block_rows(parts, queries[0].shape[0])
    bias = jnp.concatenate([bias] * GROUPS, axis=0)
    every_query = jnp.concatenate([ref[...].astype(jnp.float32) for ref in queries], axis=0).astype(jnp.bfloat16)
    scores = []
    for head in range(KV_HEADS):
        query = jnp.concatenate([every_query[:, HEADS[head * GROUPS + g]] for g in range(GROUPS)], axis=0)
        keys = jnp.concatenate([part[:, HEADS[head]] for part in key_parts], axis=0)
        products = lax.dot_general(query, keys, NT, preferred_element_type=jnp.float32)
        scores.append(products * HEAD_DIM ** (-0.5) + bias)
    weights = []
    for head in range(KV_HEADS):
        maxima = jnp.max(scores[head], axis=1, keepdims=True)
        if maxima_before is not None:
            maxima = jnp.maximum(maxima, maxima_before[head])
        exps = jnp.exp(scores[head] - across(maxima, scores[head].shape[1]))
        weights.append((exps.astype(jnp.bfloat16), maxima, jnp.sum(exps, axis=1, keepdims=True)))
    for head, (rounded, maxima, masses) in enumerate(weights):
        values = jnp.concatenate([part[:, HEADS[head]] for part in value_parts], axis=0)
        yield head, maxima, masses, jnp.dot(rounded, values, preferred_element_type=jnp.float32)


def early_kernel(owners, count, slab, *refs):
    queries, refs, (maxima_out, masses_out, weighted_out) = refs[:owners], refs[owners:-3], refs[-3:]
    bundle, last_rest, bias_ref = refs
    parts = bundle_parts(bundle, last_rest, count, slab, queries[0].shape[0])
    for head, maxima, masses, weighted in attend(queries, parts, bias_ref[...], None):
        maxima_out[head] = jnp.broadcast_to(maxima, weighted.shape)
        masses_out[head] = jnp.broadcast_to(masses, weighted.shape)
        weighted_out[head] = weighted


def late_kernel(owners, count, slab, *refs):
    queries, outs, refs = refs[:owners], refs[-owners:], refs[owners:-owners]
    bundle, last_rest, bias_ref, maxima_in, masses_in, weighted_in = refs
    local_rows = queries[0].shape[0]
    parts = bundle_parts(bundle, last_rest, count, slab, local_rows)
    rows = owners * local_rows
    lane = lax.broadcasted_iota(jnp.int32, (rows, LANES), 1)
    stats = jnp.zeros((rows, LANES), jnp.float32)
    for head, maxima, masses, weighted in attend(queries, parts, bias_ref[...], maxima_in):
        shrink = jnp.exp(maxima_in[head] - maxima)
        masses = masses + masses_in[head] * shrink
        weighted = (weighted + weighted_in[head] * shrink) * (1.0 / masses)
        level = maxima + jnp.log(masses)
        for g in range(GROUPS):
            query_head = head * GROUPS + g
            here = (lane % STRIDE == query_head) & (lane < 3 * STRIDE)
            stats = jnp.where(here, level[g * rows : (g + 1) * rows], stats)
            for owner in range(owners):
                first = g * rows + owner * local_rows
                outs[owner][:, HEADS[query_head]] = weighted[first : first + local_rows].astype(jnp.bfloat16)
    high = stats.astype(jnp.bfloat16).astype(jnp.float32)
    left = stats - high
    middle = left.astype(jnp.bfloat16).astype(jnp.float32)
    low = left - middle
    sent = jnp.where(lane < STRIDE, high, jnp.where(lane < 2 * STRIDE, middle, low))
    for owner in range(owners):
        outs[owner][:, WIDTH:] = sent[owner * local_rows : (owner + 1) * local_rows].astype(jnp.bfloat16)


def merge_kernel(*refs):
    parts, out = refs[:-1], refs[-1]
    levels = []
    for part in parts:
        terms = part[:, WIDTH:].astype(jnp.float32)
        levels.append(terms + pltpu.roll(terms, LANES - STRIDE, 1) + pltpu.roll(terms, LANES - 2 * STRIDE, 1))
    top = functools.reduce(jnp.maximum, levels)
    shares = [jnp.exp(level - top) for level in levels]
    whole = 1.0 / functools.reduce(jnp.add, shares)
    shares = [share * whole for share in shares]
    for head in range(QUERY_HEADS):
        total = functools.reduce(
            jnp.add,
            [
                share[:, head : head + 1] * part[:, HEADS[head]].astype(jnp.float32)
                for share, part in zip(shares, parts)
            ],
        )
        out[:, HEADS[head]] = total.astype(out.dtype)


def held(memory, arrays):
    return [pltpu.with_memory_space_constraint(x, memory) for x in arrays]


def swap(x, offset):
    return lax.ppermute(x, "rows", [(i, i ^ offset) for i in range(lax.axis_size("rows"))])


def after(x, *earlier):
    return lax.optimization_barrier((x, *earlier))


def shards(queries, prefix_keys, prefix_values, tree_keys, tree_values, parents):
    size = lax.axis_size("rows")
    bits = size.bit_length() - 1
    near_bits = (bits + 1) // 2
    near = 2**near_bits
    far = size // near
    local_rows = queries.shape[0]
    slab, row_width = prefix_keys.shape
    far_offsets = [near * i for i in range(far)]
    far_order = far_offsets[2:] + far_offsets[1:2]
    vmem = pl.BlockSpec(memory_space=pltpu.VMEM)
    hbm = pl.BlockSpec(memory_space=pltpu.HBM)
    params = pltpu.CompilerParams(vmem_limit_bytes=16 * 2**20)
    own_queries, own_keys, own_rest = pl.pallas_call(
        prepare_kernel,
        out_shape=[
            pltpu.VMEM(queries.shape, queries.dtype),
            pltpu.VMEM((slab, row_width), prefix_keys.dtype),
            pltpu.VMEM((slab + 2 * local_rows, row_width), prefix_keys.dtype),
        ],
        in_specs=[hbm] * 5,
        out_specs=[vmem] * 3,
        scratch_shapes=[
            pltpu.VMEM((2,) + tree_keys.shape, tree_keys.dtype),
            pltpu.SemaphoreType.DMA((5,)),
        ],
        compiler_params=params,
    )(*held(pltpu.HBM, [queries, prefix_keys, prefix_values, tree_keys, tree_values]))

    owner_offsets = [0] + far_order
    key_pieces, rest_pieces = {0: prefix_keys}, {0: own_rest}
    for bit in reversed(range(1, near_bits)):
        for offset in list(key_pieces):
            key_pieces[offset ^ (1 << bit)] = swap(key_pieces[offset], 1 << bit)
            rest_pieces[offset ^ (1 << bit)] = swap(rest_pieces[offset], 1 << bit)
    key_pieces[0] = own_keys
    block_offsets = list(key_pieces)
    sibling_offsets = [offset ^ 1 for offset in block_offsets]
    masks = [
        pl.pallas_call(
            functools.partial(mask_kernel, owner_offsets, offsets, local_rows),
            out_shape=pltpu.VMEM((far * local_rows, len(offsets) * (slab + 2 * local_rows)), jnp.float32),
            in_specs=[vmem],
            out_specs=vmem,
            compiler_params=params,
        )(parents[None, :])
        for offsets in (block_offsets, sibling_offsets)
    ]
    all_queries = {0: own_queries}
    for offset in far_order:
        sent = own_queries
        if offset == far_order[-1]:
            sent, key_pieces[near // 2] = after(sent, key_pieces[near // 2])
        all_queries[offset] = swap(sent, offset)
    gathered = [all_queries[offset] for offset in owner_offsets]
    blocks = list(key_pieces.values()) + list(rest_pieces.values())[:-1]
    bundle = pl.pallas_call(
        stack_kernel,
        out_shape=pltpu.VMEM((sum(block.shape[0] for block in blocks), row_width), prefix_keys.dtype),
        in_specs=[vmem] * len(blocks),
        out_specs=vmem,
        compiler_params=params,
    )(*held(pltpu.VMEM, blocks))
    last_rest = list(rest_pieces.values())[-1]
    far_bundle, far_rest = swap(bundle, 1), swap(last_rest, 1)
    count = len(block_offsets)
    operands = gathered + [bundle, last_rest, masks[0]]
    early_shape = (KV_HEADS, GROUPS * far * local_rows)
    state = pl.pallas_call(
        functools.partial(early_kernel, far, count, slab),
        out_shape=[
            pltpu.VMEM(early_shape + (HEAD_DIM,), jnp.float32),
        ]
        * 3,
        in_specs=[vmem] * len(operands),
        out_specs=[vmem] * 3,
        compiler_params=params,
        cost_estimate=pl.CostEstimate(flops=10999999999, bytes_accessed=36000000, transcendentals=0),
    )(*held(pltpu.VMEM, operands))
    operands = gathered + [far_bundle, far_rest, masks[1], *state]
    partials = pl.pallas_call(
        functools.partial(late_kernel, far, count, slab),
        out_shape=[pltpu.VMEM((local_rows, WIDTH + LANES), jnp.bfloat16)] * far,
        in_specs=[vmem] * len(operands),
        out_specs=[vmem] * far,
        compiler_params=params,
    )(*held(pltpu.VMEM, operands))
    parts = [partials[0]]
    for offset in far_order:
        parts.append(swap(partials[owner_offsets.index(offset)], offset))
    return pl.pallas_call(
        merge_kernel,
        out_shape=jax.ShapeDtypeStruct((local_rows, WIDTH), jnp.bfloat16),
        in_specs=[vmem] * far,
        out_specs=vmem,
        compiler_params=params,
    )(*held(pltpu.VMEM, parts))


def solution(mesh):
    placed = (
        P(("group", "rows"), None),
        P(("group", "rows"), None),
        P(("group", "rows"), None),
        P(("group", "rows"), None),
        P(("group", "rows"), None),
        P("group"),
    )
    return jax.shard_map(
        shards, mesh=mesh, in_specs=placed, out_specs=P(("group", "rows"), None), check_vma=False
    )
```

```python
import functools

import jax
import jax.numpy as jnp
from jax import lax
from jax.experimental import pallas as pl
from jax.experimental.pallas import tpu as pltpu
from jax.sharding import PartitionSpec as P

QUERY_HEADS = 24
KV_HEADS = 8
HEAD_DIM = 128
TREE_DEPTH = 4
GROUPS = QUERY_HEADS // KV_HEADS
WIDTH = QUERY_HEADS * HEAD_DIM
LANES = 128
STRIDE = 32
CHUNKS = 4
NT = (((1,), (1,)), ((), ()))
HEADS = [slice(head * HEAD_DIM, (head + 1) * HEAD_DIM) for head in range(QUERY_HEADS)]


def rest_kernel(prefix_values, tree_keys, tree_values, rest, tree_scratch, sems):
    slab = prefix_values.shape[0]
    chunk = slab // CHUNKS
    copies = [
        pltpu.make_async_copy(tree_keys, tree_scratch.at[0], sems.at[0]),
        pltpu.make_async_copy(tree_values, tree_scratch.at[1], sems.at[1]),
    ]
    for place in range(CHUNKS):
        rows = slice(place * chunk, (place + 1) * chunk)
        copies.append(pltpu.make_async_copy(prefix_values.at[rows], rest.at[rows], sems.at[2 + place]))
    for copy in copies:
        copy.start()
    for copy in copies:
        copy.wait()
    trees = [tree_scratch[0].astype(jnp.float32), tree_scratch[1].astype(jnp.float32)]
    local_rows = (rest.shape[0] - slab) // 2
    for head in range(KV_HEADS):
        rows = slice(head * local_rows, (head + 1) * local_rows)
        both = jnp.concatenate([tree[rows] for tree in trees], axis=0)
        rest[slab:, HEADS[head]] = both.astype(rest.dtype)


def stack_kernel(*refs):
    blocks, out = refs[:-1], refs[-1]
    first = 0
    for block in blocks:
        out[first : first + block.shape[0]] = block[...]
        first += block.shape[0]


def chosen(index, values):
    picked = jnp.full(index.shape, values[0], jnp.int32)
    for place in range(1, len(values)):
        picked = jnp.where(index == place, values[place], picked)
    return picked


def mask_kernel(owner_offsets, token_offsets, local_rows, parents, bias):
    position = lax.axis_index("rows")
    rows, columns = bias.shape
    block = columns // len(token_offsets)
    slab = block - 2 * local_rows
    slot = lax.broadcasted_iota(jnp.int32, (rows, 1), 0)
    walker = (position ^ chosen(slot // local_rows, owner_offsets)) * local_rows + slot % local_rows
    slot = lax.broadcasted_iota(jnp.int32, (1, columns), 1)
    within = slot % block - slab
    token = (position ^ chosen(slot // block, token_offsets)) * local_rows + within
    is_tree = (within >= 0) & (within < local_rows)
    candidates = lax.broadcasted_iota(jnp.int32, (rows, parents.shape[1]), 1)
    parent = parents[...]
    allowed = walker == token
    for _ in range(TREE_DEPTH - 1):
        walker = jnp.sum(jnp.where(walker == candidates, parent, 0), axis=1, keepdims=True)
        allowed = allowed | (walker == token)
    bias[...] = jnp.where((allowed & is_tree) | (within < 0), 0.0, -jnp.inf)


def block_rows(parts, local_rows):
    keys, values = [], []
    for slab_keys, rest in parts:
        slab = slab_keys.shape[0]
        tree = rest[slab:]
        halves = tree.astype(jnp.float32)
        turned = jnp.concatenate([halves[local_rows:], halves[:local_rows]], axis=0)
        keys += [slab_keys[...], tree]
        values += [rest[:slab], turned.astype(jnp.bfloat16)]
    return keys, values


def bundle_parts(bundle, last_rest, count, slab, local_rows):
    block = slab + 2 * local_rows
    rests = [bundle.at[count * slab + i * block : count * slab + (i + 1) * block] for i in range(count - 1)]
    return [(bundle.at[i * slab : (i + 1) * slab], rest) for i, rest in enumerate(rests + [last_rest])]


def rows_kernel(*refs):
    blocks, out = refs[:-1], refs[-1]
    rows = blocks[0].shape[0]
    for place in range(0, len(blocks), 2):
        both = [block[...].astype(jnp.float32) for block in blocks[place : place + 2]]
        out[place * rows : (place + 2) * rows] = jnp.concatenate(both, axis=0).astype(out.dtype)


def attend_kernel(owners, count, slab, queries, near_bundle, near_rest, far_bundle, far_rest, bias_ref, *outs):
    rows = queries.shape[0]
    local_rows = rows // owners
    parts = bundle_parts(near_bundle, near_rest, count, slab, local_rows)
    parts += bundle_parts(far_bundle, far_rest, count, slab, local_rows)
    key_parts, value_parts = block_rows(parts, local_rows)
    bias = jnp.concatenate([bias_ref[...]] * GROUPS, axis=0)
    scores = []
    for head in range(KV_HEADS):
        query = jnp.concatenate([queries[:, HEADS[head * GROUPS + g]] for g in range(GROUPS)], axis=0)
        keys = jnp.concatenate([part[:, HEADS[head]] for part in key_parts], axis=0)
        products = lax.dot_general(query, keys, NT, preferred_element_type=jnp.float32)
        scores.append(products * HEAD_DIM ** (-0.5) + bias)
    weights = []
    for head in range(KV_HEADS):
        maxima = jnp.max(scores[head], axis=1, keepdims=True)
        exps = jnp.exp(scores[head] - maxima)
        masses = jnp.sum(exps, axis=1, keepdims=True)
        weights.append((exps.astype(jnp.bfloat16), maxima + jnp.log(masses), 1.0 / masses))
    lane = lax.broadcasted_iota(jnp.int32, (rows, LANES), 1)
    stats = jnp.zeros((rows, LANES), jnp.float32)
    for head, (rounded, level, inverse) in enumerate(weights):
        values = jnp.concatenate([part[:, HEADS[head]] for part in value_parts], axis=0)
        weighted = jnp.dot(rounded, values, preferred_element_type=jnp.float32) * inverse
        for g in range(GROUPS):
            query_head = head * GROUPS + g
            here = (lane % STRIDE == query_head) & (lane < 3 * STRIDE)
            stats = jnp.where(here, level[g * rows : (g + 1) * rows], stats)
            for owner in range(owners):
                first = g * rows + owner * local_rows
                outs[owner][:, HEADS[query_head]] = weighted[first : first + local_rows].astype(jnp.bfloat16)
    high = stats.astype(jnp.bfloat16).astype(jnp.float32)
    left = stats - high
    middle = left.astype(jnp.bfloat16).astype(jnp.float32)
    low = left - middle
    sent = jnp.where(lane < STRIDE, high, jnp.where(lane < 2 * STRIDE, middle, low))
    for owner in range(owners):
        outs[owner][:, WIDTH:] = sent[owner * local_rows : (owner + 1) * local_rows].astype(jnp.bfloat16)


def merge_kernel(*refs):
    parts, out = refs[:-1], refs[-1]
    levels = []
    for part in parts:
        terms = part[:, WIDTH:].astype(jnp.float32)
        levels.append(terms + pltpu.roll(terms, LANES - STRIDE, 1) + pltpu.roll(terms, LANES - 2 * STRIDE, 1))
    top = functools.reduce(jnp.maximum, levels)
    shares = [jnp.exp(level - top) for level in levels]
    whole = 1.0 / functools.reduce(jnp.add, shares)
    shares = [share * whole for share in shares]
    for head in range(QUERY_HEADS):
        total = functools.reduce(
            jnp.add,
            [
                share[:, head : head + 1] * part[:, HEADS[head]].astype(jnp.float32)
                for share, part in zip(shares, parts)
            ],
        )
        out[:, HEADS[head]] = total.astype(out.dtype)


def held(memory, arrays):
    return [pltpu.with_memory_space_constraint(x, memory) for x in arrays]


def swap(x, offset):
    return lax.ppermute(x, "rows", [(i, i ^ offset) for i in range(lax.axis_size("rows"))])


def by_head(x):
    return jnp.transpose(x.reshape(-1, KV_HEADS, HEAD_DIM), (1, 0, 2)).reshape(-1, HEAD_DIM)


def after(x, *earlier):
    return lax.optimization_barrier((x, *earlier))


def shards(queries, prefix_keys, prefix_values, tree_keys, tree_values, parents):
    size = lax.axis_size("rows")
    bits = size.bit_length() - 1
    near_bits = (bits + 1) // 2
    near = 2**near_bits
    far = size // near
    local_rows = queries.shape[0]
    slab, row_width = prefix_keys.shape
    far_offsets = [near * i for i in range(far)]
    far_order = far_offsets[:0:-1]
    vmem = pl.BlockSpec(memory_space=pltpu.VMEM)
    hbm = pl.BlockSpec(memory_space=pltpu.HBM)
    params = pltpu.CompilerParams(vmem_limit_bytes=16 * 2**20)
    own_rest = pl.pallas_call(
        rest_kernel,
        out_shape=pltpu.VMEM((slab + 2 * local_rows, row_width), prefix_values.dtype),
        in_specs=[hbm] * 3,
        out_specs=vmem,
        scratch_shapes=[
            pltpu.VMEM((2, KV_HEADS * local_rows, HEAD_DIM), tree_keys.dtype),
            pltpu.SemaphoreType.DMA((2 + CHUNKS,)),
        ],
        compiler_params=params,
    )(*held(pltpu.HBM, [prefix_values, by_head(tree_keys), by_head(tree_values)]))

    owner_offsets = [0] + far_order
    key_pieces, rest_pieces = {0: prefix_keys}, {0: own_rest}
    for bit in reversed(range(1, near_bits)):
        for offset in list(key_pieces):
            key_pieces[offset ^ (1 << bit)] = swap(key_pieces[offset], 1 << bit)
            rest_pieces[offset ^ (1 << bit)] = swap(rest_pieces[offset], 1 << bit)
    block_offsets = list(key_pieces)
    sibling_offsets = [offset ^ 1 for offset in block_offsets]
    mask = pl.pallas_call(
        functools.partial(mask_kernel, owner_offsets, block_offsets + sibling_offsets, local_rows),
        out_shape=pltpu.VMEM((far * local_rows, near * (slab + 2 * local_rows)), jnp.float32),
        in_specs=[vmem],
        out_specs=vmem,
        compiler_params=params,
    )(parents[None, :])
    all_queries = {0: queries}
    for offset in far_order:
        sent = queries
        if offset == far_order[-1]:
            sent, key_pieces[near // 2] = after(sent, key_pieces[near // 2])
        all_queries[offset] = swap(sent, offset)
    gathered = pl.pallas_call(
        rows_kernel,
        out_shape=pltpu.VMEM((far * local_rows, WIDTH), queries.dtype),
        in_specs=[vmem] * far,
        out_specs=vmem,
        compiler_params=params,
        cost_estimate=pl.CostEstimate(flops=10999999999, bytes_accessed=36000000, transcendentals=0),
    )(*held(pltpu.VMEM, [all_queries[offset] for offset in owner_offsets]))
    blocks = list(key_pieces.values()) + list(rest_pieces.values())[:-1]
    bundle = pl.pallas_call(
        stack_kernel,
        out_shape=pltpu.VMEM((sum(block.shape[0] for block in blocks), row_width), prefix_keys.dtype),
        in_specs=[vmem] * len(blocks),
        out_specs=vmem,
        compiler_params=params,
    )(*held(pltpu.VMEM, blocks))
    last_rest = list(rest_pieces.values())[-1]
    far_bundle, far_rest = swap(bundle, 1), swap(last_rest, 1)
    count = len(block_offsets)
    operands = [gathered, bundle, last_rest, far_bundle, far_rest, mask]
    partials = pl.pallas_call(
        functools.partial(attend_kernel, far, count, slab),
        out_shape=[pltpu.VMEM((local_rows, WIDTH + LANES), jnp.bfloat16)] * far,
        in_specs=[vmem] * len(operands),
        out_specs=[vmem] * far,
        compiler_params=params,
    )(*held(pltpu.VMEM, operands))
    parts = [partials[0]]
    for offset in far_offsets[2:] + far_offsets[1:2]:
        parts.append(swap(partials[owner_offsets.index(offset)], offset))
    return pl.pallas_call(
        merge_kernel,
        out_shape=jax.ShapeDtypeStruct((local_rows, WIDTH), jnp.bfloat16),
        in_specs=[vmem] * far,
        out_specs=vmem,
        compiler_params=params,
    )(*held(pltpu.VMEM, parts))


def solution(mesh):
    placed = (
        P(("group", "rows"), None),
        P(("group", "rows"), None),
        P(("group", "rows"), None),
        P(("group", "rows"), None),
        P(("group", "rows"), None),
        P("group"),
    )
    return jax.shard_map(
        shards, mesh=mesh, in_specs=placed, out_specs=P(("group", "rows"), None), check_vma=False
    )
```

```python
import functools

import jax
import jax.numpy as jnp
from jax import lax
from jax.experimental import pallas as pl
from jax.experimental.pallas import tpu as pltpu
from jax.sharding import PartitionSpec as P

QUERY_HEADS = 24
KV_HEADS = 8
HEAD_DIM = 128
TREE_DEPTH = 4
GROUPS = QUERY_HEADS // KV_HEADS
WIDTH = QUERY_HEADS * HEAD_DIM
LANES = 128
STRIDE = 32
CHUNKS = 4
NT = (((1,), (1,)), ((), ()))
HEADS = [slice(head * HEAD_DIM, (head + 1) * HEAD_DIM) for head in range(QUERY_HEADS)]


def rest_kernel(prefix_values, tree_keys, tree_values, rest, tree_scratch, sems):
    slab = prefix_values.shape[0]
    chunk = slab // CHUNKS
    copies = [
        pltpu.make_async_copy(tree_keys, tree_scratch.at[0], sems.at[0]),
        pltpu.make_async_copy(tree_values, tree_scratch.at[1], sems.at[1]),
    ]
    for place in range(CHUNKS):
        rows = slice(place * chunk, (place + 1) * chunk)
        copies.append(pltpu.make_async_copy(prefix_values.at[rows], rest.at[rows], sems.at[2 + place]))
    for copy in copies:
        copy.start()
    for copy in copies:
        copy.wait()
    trees = [tree_scratch[0].astype(jnp.float32), tree_scratch[1].astype(jnp.float32)]
    local_rows = (rest.shape[0] - slab) // 2
    for head in range(KV_HEADS):
        rows = slice(head * local_rows, (head + 1) * local_rows)
        both = jnp.concatenate([tree[rows] for tree in trees], axis=0)
        rest[slab:, HEADS[head]] = both.astype(rest.dtype)


def stack_kernel(*refs):
    blocks, out = refs[:-1], refs[-1]
    first = 0
    for block in blocks:
        out[first : first + block.shape[0]] = block[...]
        first += block.shape[0]


def chosen(index, values):
    picked = jnp.full(index.shape, values[0], jnp.int32)
    for place in range(1, len(values)):
        picked = jnp.where(index == place, values[place], picked)
    return picked


def mask_kernel(owner_offsets, token_offsets, local_rows, parents, bias):
    position = lax.axis_index("rows")
    rows, columns = bias.shape
    block = columns // len(token_offsets)
    slab = block - 2 * local_rows
    slot = lax.broadcasted_iota(jnp.int32, (rows, 1), 0)
    walker = (position ^ chosen(slot // local_rows, owner_offsets)) * local_rows + slot % local_rows
    slot = lax.broadcasted_iota(jnp.int32, (1, columns), 1)
    within = slot % block - slab
    token = (position ^ chosen(slot // block, token_offsets)) * local_rows + within
    is_tree = (within >= 0) & (within < local_rows)
    candidates = lax.broadcasted_iota(jnp.int32, (rows, parents.shape[1]), 1)
    parent = parents[...]
    allowed = walker == token
    for _ in range(TREE_DEPTH - 1):
        walker = jnp.sum(jnp.where(walker == candidates, parent, 0), axis=1, keepdims=True)
        allowed = allowed | (walker == token)
    bias[...] = jnp.where((allowed & is_tree) | (within < 0), 0.0, -jnp.inf)


def block_rows(parts, local_rows):
    keys, values = [], []
    for slab_keys, rest in parts:
        slab = slab_keys.shape[0]
        tree = rest[slab:]
        halves = tree.astype(jnp.float32)
        turned = jnp.concatenate([halves[local_rows:], halves[:local_rows]], axis=0)
        keys += [slab_keys[...], tree]
        values += [rest[:slab], turned.astype(jnp.bfloat16)]
    return keys, values


def bundle_parts(bundle, last_rest, count, slab, local_rows):
    block = slab + 2 * local_rows
    rests = [bundle.at[count * slab + i * block : count * slab + (i + 1) * block] for i in range(count - 1)]
    return [(bundle.at[i * slab : (i + 1) * slab], rest) for i, rest in enumerate(rests + [last_rest])]


def rows_kernel(*refs):
    blocks, out = refs[:-1], refs[-1]
    rows = blocks[0].shape[0]
    for place in range(0, len(blocks), 2):
        both = [block[...].astype(jnp.float32) for block in blocks[place : place + 2]]
        out[place * rows : (place + 2) * rows] = jnp.concatenate(both, axis=0).astype(out.dtype)


def attend_kernel(owners, count, slab, queries, near_bundle, near_rest, far_bundle, far_rest, bias_ref, *outs):
    rows = queries.shape[0]
    local_rows = rows // owners
    parts = bundle_parts(near_bundle, near_rest, count, slab, local_rows)
    parts += bundle_parts(far_bundle, far_rest, count, slab, local_rows)
    key_parts, value_parts = block_rows(parts, local_rows)
    bias = jnp.concatenate([bias_ref[...]] * GROUPS, axis=0)
    scores = []
    for head in range(KV_HEADS):
        query = jnp.concatenate([queries[:, HEADS[head * GROUPS + g]] for g in range(GROUPS)], axis=0)
        keys = jnp.concatenate([part[:, HEADS[head]] for part in key_parts], axis=0)
        products = lax.dot_general(query, keys, NT, preferred_element_type=jnp.float32)
        scores.append(products * HEAD_DIM ** (-0.5) + bias)
    weights = []
    for head in range(KV_HEADS):
        maxima = jnp.max(scores[head], axis=1, keepdims=True)
        exps = jnp.exp(scores[head] - maxima)
        masses = jnp.sum(exps, axis=1, keepdims=True)
        weights.append((exps.astype(jnp.bfloat16), maxima + jnp.log(masses), 1.0 / masses))
    lane = lax.broadcasted_iota(jnp.int32, (rows, LANES), 1)
    stats = jnp.zeros((rows, LANES), jnp.float32)
    for head, (rounded, level, inverse) in enumerate(weights):
        values = jnp.concatenate([part[:, HEADS[head]] for part in value_parts], axis=0)
        weighted = jnp.dot(rounded, values, preferred_element_type=jnp.float32) * inverse
        for g in range(GROUPS):
            query_head = head * GROUPS + g
            here = (lane % STRIDE == query_head) & (lane < 3 * STRIDE)
            stats = jnp.where(here, level[g * rows : (g + 1) * rows], stats)
            for owner in range(owners):
                first = g * rows + owner * local_rows
                outs[owner][:, HEADS[query_head]] = weighted[first : first + local_rows].astype(jnp.bfloat16)
    high = stats.astype(jnp.bfloat16).astype(jnp.float32)
    left = stats - high
    middle = left.astype(jnp.bfloat16).astype(jnp.float32)
    low = left - middle
    sent = jnp.where(lane < STRIDE, high, jnp.where(lane < 2 * STRIDE, middle, low))
    for owner in range(owners):
        outs[owner][:, WIDTH:] = sent[owner * local_rows : (owner + 1) * local_rows].astype(jnp.bfloat16)


def merge_kernel(*refs):
    parts, out = refs[:-1], refs[-1]
    levels = []
    for part in parts:
        terms = part[:, WIDTH:].astype(jnp.float32)
        levels.append(terms + pltpu.roll(terms, LANES - STRIDE, 1) + pltpu.roll(terms, LANES - 2 * STRIDE, 1))
    top = functools.reduce(jnp.maximum, levels)
    shares = [jnp.exp(level - top) for level in levels]
    whole = 1.0 / functools.reduce(jnp.add, shares)
    shares = [share * whole for share in shares]
    for head in range(QUERY_HEADS):
        total = functools.reduce(
            jnp.add,
            [
                share[:, head : head + 1] * part[:, HEADS[head]].astype(jnp.float32)
                for share, part in zip(shares, parts)
            ],
        )
        out[:, HEADS[head]] = total.astype(out.dtype)


def held(memory, arrays):
    return [pltpu.with_memory_space_constraint(x, memory) for x in arrays]


def swap(x, offset):
    return lax.ppermute(x, "rows", [(i, i ^ offset) for i in range(lax.axis_size("rows"))])


def by_head(x):
    return jnp.transpose(x.reshape(-1, KV_HEADS, HEAD_DIM), (1, 0, 2)).reshape(-1, HEAD_DIM)


def after(x, *earlier):
    return lax.optimization_barrier((x, *earlier))


def shards(queries, prefix_keys, prefix_values, tree_keys, tree_values, parents):
    size = lax.axis_size("rows")
    bits = size.bit_length() - 1
    near_bits = (bits + 1) // 2
    near = 2**near_bits
    far = size // near
    local_rows = queries.shape[0]
    slab, row_width = prefix_keys.shape
    far_offsets = [0] + [near * i | 1 for i in range(1, far)]
    far_order = far_offsets[2:] + far_offsets[1:2]
    vmem = pl.BlockSpec(memory_space=pltpu.VMEM)
    hbm = pl.BlockSpec(memory_space=pltpu.HBM)
    params = pltpu.CompilerParams(vmem_limit_bytes=16 * 2**20)
    own_rest = pl.pallas_call(
        rest_kernel,
        out_shape=pltpu.VMEM((slab + 2 * local_rows, row_width), prefix_values.dtype),
        in_specs=[hbm] * 3,
        out_specs=vmem,
        scratch_shapes=[
            pltpu.VMEM((2, KV_HEADS * local_rows, HEAD_DIM), tree_keys.dtype),
            pltpu.SemaphoreType.DMA((2 + CHUNKS,)),
        ],
        compiler_params=params,
    )(*held(pltpu.HBM, [prefix_values, by_head(tree_keys), by_head(tree_values)]))

    owner_offsets = [0] + far_order
    key_pieces, rest_pieces = {0: prefix_keys}, {0: own_rest}
    for bit in reversed(range(1, near_bits)):
        for offset in list(key_pieces):
            step = 1 << bit
            key_pieces[offset ^ step] = swap(key_pieces[offset], step)
            rest_pieces[offset ^ step] = swap(rest_pieces[offset], step)
    block_offsets = list(key_pieces)
    sibling_offsets = [offset ^ 1 for offset in block_offsets]
    mask = pl.pallas_call(
        functools.partial(mask_kernel, owner_offsets, block_offsets + sibling_offsets, local_rows),
        out_shape=pltpu.VMEM((far * local_rows, near * (slab + 2 * local_rows)), jnp.float32),
        in_specs=[vmem],
        out_specs=vmem,
        compiler_params=params,
    )(parents[None, :])
    all_queries = {0: queries}
    for offset in far_order:
        sent = queries
        if offset == far_order[-1]:
            sent, key_pieces[block_offsets[-1]] = after(sent, key_pieces[block_offsets[-1]])
        all_queries[offset] = swap(sent, offset)
    gathered = pl.pallas_call(
        rows_kernel,
        out_shape=pltpu.VMEM((far * local_rows, WIDTH), queries.dtype),
        in_specs=[vmem] * far,
        out_specs=vmem,
        compiler_params=params,
        cost_estimate=pl.CostEstimate(flops=10999999999, bytes_accessed=36000000, transcendentals=0),
    )(*held(pltpu.VMEM, [all_queries[offset] for offset in owner_offsets]))
    blocks = list(key_pieces.values()) + list(rest_pieces.values())[:-1]
    bundle = pl.pallas_call(
        stack_kernel,
        out_shape=pltpu.VMEM((sum(block.shape[0] for block in blocks), row_width), prefix_keys.dtype),
        in_specs=[vmem] * len(blocks),
        out_specs=vmem,
        compiler_params=params,
    )(*held(pltpu.VMEM, blocks))
    last_rest = list(rest_pieces.values())[-1]
    far_bundle, far_rest = swap(bundle, 1), swap(last_rest, 1)
    count = len(block_offsets)
    operands = [gathered, bundle, last_rest, far_bundle, far_rest, mask]
    partials = pl.pallas_call(
        functools.partial(attend_kernel, far, count, slab),
        out_shape=[pltpu.VMEM((local_rows, WIDTH + LANES), jnp.bfloat16)] * far,
        in_specs=[vmem] * len(operands),
        out_specs=[vmem] * far,
        compiler_params=params,
    )(*held(pltpu.VMEM, operands))
    parts = [partials[0]]
    for offset in far_offsets[-1:] + far_offsets[1:-1]:
        parts.append(swap(partials[owner_offsets.index(offset)], offset))
    return pl.pallas_call(
        merge_kernel,
        out_shape=jax.ShapeDtypeStruct((local_rows, WIDTH), jnp.bfloat16),
        in_specs=[vmem] * far,
        out_specs=vmem,
        compiler_params=params,
    )(*held(pltpu.VMEM, parts))


def solution(mesh):
    placed = (
        P(("group", "rows"), None),
        P(("group", "rows"), None),
        P(("group", "rows"), None),
        P(("group", "rows"), None),
        P(("group", "rows"), None),
        P("group"),
    )
    return jax.shard_map(
        shards, mesh=mesh, in_specs=placed, out_specs=P(("group", "rows"), None), check_vma=False
    )
```

```python
import functools

import jax
import jax.numpy as jnp
from jax import lax
from jax.experimental import pallas as pl
from jax.experimental.pallas import tpu as pltpu
from jax.sharding import PartitionSpec as P

QUERY_HEADS = 24
KV_HEADS = 8
HEAD_DIM = 128
TREE_DEPTH = 4
GROUPS = QUERY_HEADS // KV_HEADS
WIDTH = QUERY_HEADS * HEAD_DIM
LANES = 128
STRIDE = 32
NT = (((1,), (1,)), ((), ()))
SCHEDULE_LAST = pl.CostEstimate(flops=3 * 10**10, bytes_accessed=10**8, transcendentals=0)
HEADS = [slice(head * HEAD_DIM, (head + 1) * HEAD_DIM) for head in range(QUERY_HEADS)]


def rest_kernel(prefix_values, tree_keys, tree_values, rest, tree_scratch, sems):
    slab = prefix_values.shape[0]
    copies = [
        pltpu.make_async_copy(tree_keys, tree_scratch.at[0], sems.at[0]),
        pltpu.make_async_copy(tree_values, tree_scratch.at[1], sems.at[1]),
        pltpu.make_async_copy(prefix_values, rest.at[:slab], sems.at[2]),
    ]
    for copy in copies:
        copy.start()
    for copy in copies:
        copy.wait()
    trees = [tree_scratch[0].astype(jnp.float32), tree_scratch[1].astype(jnp.float32)]
    local_rows = (rest.shape[0] - slab) // 2
    for head in range(KV_HEADS):
        rows = slice(head * local_rows, (head + 1) * local_rows)
        both = jnp.concatenate([tree[rows] for tree in trees], axis=0)
        rest[slab:, HEADS[head]] = both.astype(rest.dtype)


def stack_kernel(*refs):
    blocks, out = refs[:-1], refs[-1]
    first = 0
    for block in blocks:
        out[first : first + block.shape[0]] = block[...]
        first += block.shape[0]


def chosen(index, values):
    picked = jnp.full(index.shape, values[0], jnp.int32)
    for place in range(1, len(values)):
        picked = jnp.where(index == place, values[place], picked)
    return picked


def mask_kernel(owner_offsets, token_offsets, local_rows, parents, bias):
    position = lax.axis_index("rows")
    rows, columns = bias.shape
    block = columns // len(token_offsets)
    slab = block - 2 * local_rows
    slot = lax.broadcasted_iota(jnp.int32, (rows, 1), 0)
    walker = (position ^ chosen(slot // local_rows, owner_offsets)) * local_rows + slot % local_rows
    slot = lax.broadcasted_iota(jnp.int32, (1, columns), 1)
    within = slot % block - slab
    token = (position ^ chosen(slot // block, token_offsets)) * local_rows + within
    is_tree = (within >= 0) & (within < local_rows)
    candidates = lax.broadcasted_iota(jnp.int32, (rows, parents.shape[1]), 1)
    parent = parents[...]
    allowed = walker == token
    for _ in range(TREE_DEPTH - 1):
        walker = jnp.sum(jnp.where(walker == candidates, parent, 0), axis=1, keepdims=True)
        allowed = allowed | (walker == token)
    bias[...] = jnp.where((allowed & is_tree) | (within < 0), 0.0, -jnp.inf)


def block_rows(parts, local_rows):
    keys, values = [], []
    for slab_keys, rest in parts:
        slab = slab_keys.shape[0]
        tree = rest[slab:]
        halves = tree.astype(jnp.float32)
        turned = jnp.concatenate([halves[local_rows:], halves[:local_rows]], axis=0)
        keys += [slab_keys[...], tree]
        values += [rest[:slab], turned.astype(jnp.bfloat16)]
    return keys, values


def bundle_parts(bundle, last_rest, count, slab, local_rows):
    block = slab + 2 * local_rows
    rests = [bundle.at[count * slab + i * block : count * slab + (i + 1) * block] for i in range(count - 1)]
    return [(bundle.at[i * slab : (i + 1) * slab], rest) for i, rest in enumerate(rests + [last_rest])]


def rows_kernel(*refs):
    blocks, out = refs[:-1], refs[-1]
    rows = blocks[0].shape[0]
    for place in range(0, len(blocks), 2):
        both = [block[...].astype(jnp.float32) for block in blocks[place : place + 2]]
        out[place * rows : (place + 2) * rows] = jnp.concatenate(both, axis=0).astype(out.dtype)


def attend_kernel(owners, count, slab, queries, near_bundle, near_rest, far_bundle, far_rest, bias_ref, *outs):
    rows = queries.shape[0]
    local_rows = rows // owners
    parts = bundle_parts(near_bundle, near_rest, count, slab, local_rows)
    parts += bundle_parts(far_bundle, far_rest, count, slab, local_rows)
    key_parts, value_parts = block_rows(parts, local_rows)
    bias = jnp.concatenate([bias_ref[...]] * GROUPS, axis=0)
    scores = []
    for head in range(KV_HEADS):
        query = jnp.concatenate([queries[:, HEADS[head * GROUPS + g]] for g in range(GROUPS)], axis=0)
        keys = jnp.concatenate([part[:, HEADS[head]] for part in key_parts], axis=0)
        products = lax.dot_general(query, keys, NT, preferred_element_type=jnp.float32)
        scores.append(products * HEAD_DIM ** (-0.5) + bias)
    weights = []
    for head in range(KV_HEADS):
        maxima = jnp.max(scores[head], axis=1, keepdims=True)
        exps = jnp.exp(scores[head] - maxima)
        masses = jnp.sum(exps, axis=1, keepdims=True)
        weights.append((exps.astype(jnp.bfloat16), maxima + jnp.log(masses), 1.0 / masses))
    lane = lax.broadcasted_iota(jnp.int32, (rows, LANES), 1)
    stats = jnp.zeros((rows, LANES), jnp.float32)
    for head, (rounded, level, inverse) in enumerate(weights):
        values = jnp.concatenate([part[:, HEADS[head]] for part in value_parts], axis=0)
        weighted = jnp.dot(rounded, values, preferred_element_type=jnp.float32) * inverse
        for g in range(GROUPS):
            query_head = head * GROUPS + g
            here = (lane % STRIDE == query_head) & (lane < 3 * STRIDE)
            stats = jnp.where(here, level[g * rows : (g + 1) * rows], stats)
            for owner in range(owners):
                first = g * rows + owner * local_rows
                outs[owner][:, HEADS[query_head]] = weighted[first : first + local_rows].astype(outs[owner].dtype)
    high = stats.astype(jnp.bfloat16).astype(jnp.float32)
    left = stats - high
    middle = left.astype(jnp.bfloat16).astype(jnp.float32)
    low = left - middle
    sent = jnp.where(lane < STRIDE, high, jnp.where(lane < 2 * STRIDE, middle, low))
    for owner in range(owners):
        outs[owner][:, WIDTH:] = sent[owner * local_rows : (owner + 1) * local_rows].astype(outs[owner].dtype)


def merge_kernel(*refs):
    parts, out = refs[:-1], refs[-1]
    levels = []
    for part in parts:
        terms = part[:, WIDTH:].astype(jnp.float32)
        levels.append(terms + pltpu.roll(terms, LANES - STRIDE, 1) + pltpu.roll(terms, LANES - 2 * STRIDE, 1))
    top = functools.reduce(jnp.maximum, levels)
    shares = [jnp.exp(level - top) for level in levels]
    whole = 1.0 / functools.reduce(jnp.add, shares)
    shares = [share * whole for share in shares]
    for head in range(QUERY_HEADS):
        own = parts[0][:, HEADS[head]].astype(jnp.float32)
        total = own
        for share, part in zip(shares[1:], parts[1:]):
            total = total + share[:, head : head + 1] * (part[:, HEADS[head]].astype(jnp.float32) - own)
        out[:, HEADS[head]] = total.astype(out.dtype)


def held(memory, arrays):
    return [pltpu.with_memory_space_constraint(x, memory) for x in arrays]


def swap(x, offset):
    return lax.ppermute(x, "rows", [(i, i ^ offset) for i in range(lax.axis_size("rows"))])


def by_head(x):
    return jnp.transpose(x.reshape(-1, KV_HEADS, HEAD_DIM), (1, 0, 2)).reshape(-1, HEAD_DIM)


def after(x, *earlier):
    return lax.optimization_barrier((x, *earlier))


def shards(queries, prefix_keys, prefix_values, tree_keys, tree_values, parents):
    size = lax.axis_size("rows")
    bits = size.bit_length() - 1
    near_bits = (bits + 1) // 2
    near = 2**near_bits
    far = size // near
    local_rows = queries.shape[0]
    slab, row_width = prefix_keys.shape
    far_offsets = [0] + [near * i | 1 for i in range(1, far)]
    far_order = far_offsets[2:] + far_offsets[1:2]
    vmem = pl.BlockSpec(memory_space=pltpu.VMEM)
    hbm = pl.BlockSpec(memory_space=pltpu.HBM)
    params = pltpu.CompilerParams(vmem_limit_bytes=16 * 2**20)
    own_rest = pl.pallas_call(
        rest_kernel,
        out_shape=pltpu.VMEM((slab + 2 * local_rows, row_width), prefix_values.dtype),
        in_specs=[hbm] * 3,
        out_specs=vmem,
        scratch_shapes=[
            pltpu.VMEM((2, KV_HEADS * local_rows, HEAD_DIM), tree_keys.dtype),
            pltpu.SemaphoreType.DMA((3,)),
        ],
        compiler_params=params,
    )(*held(pltpu.HBM, [prefix_values, by_head(tree_keys), by_head(tree_values)]))

    owner_offsets = [0] + far_order
    key_pieces, rest_pieces = {0: prefix_keys}, {0: own_rest}
    for bit in reversed(range(1, near_bits)):
        for offset in list(key_pieces):
            step = 1 << bit
            key_pieces[offset ^ step] = swap(key_pieces[offset], step)
            rest_pieces[offset ^ step] = swap(rest_pieces[offset], step)
    block_offsets = list(key_pieces)
    sibling_offsets = [offset ^ 1 for offset in block_offsets]
    mask = pl.pallas_call(
        functools.partial(mask_kernel, owner_offsets, block_offsets + sibling_offsets, local_rows),
        out_shape=pltpu.VMEM((far * local_rows, near * (slab + 2 * local_rows)), jnp.float32),
        in_specs=[vmem],
        out_specs=vmem,
        compiler_params=params,
    )(parents[None, :])
    all_queries = {0: queries}
    for offset in far_order:
        sent = queries
        if offset == far_order[-1]:
            sent, key_pieces[block_offsets[-1]] = after(sent, key_pieces[block_offsets[-1]])
        all_queries[offset] = swap(sent, offset)
    gathered = pl.pallas_call(
        rows_kernel,
        out_shape=pltpu.VMEM((far * local_rows, WIDTH), queries.dtype),
        in_specs=[vmem] * far,
        out_specs=vmem,
        compiler_params=params,
        cost_estimate=SCHEDULE_LAST,
    )(*held(pltpu.VMEM, [all_queries[offset] for offset in owner_offsets]))
    blocks = list(key_pieces.values()) + list(rest_pieces.values())[:-1]
    bundle = pl.pallas_call(
        stack_kernel,
        out_shape=pltpu.VMEM((sum(block.shape[0] for block in blocks), row_width), prefix_keys.dtype),
        in_specs=[vmem] * len(blocks),
        out_specs=vmem,
        compiler_params=params,
    )(*held(pltpu.VMEM, blocks))
    last_rest = list(rest_pieces.values())[-1]
    far_bundle, far_rest = swap(bundle, 1), swap(last_rest, 1)
    count = len(block_offsets)
    operands = [gathered, bundle, last_rest, far_bundle, far_rest, mask]
    partials = pl.pallas_call(
        functools.partial(attend_kernel, far, count, slab),
        out_shape=[
            pltpu.VMEM((local_rows, WIDTH + LANES), jnp.bfloat16 if offset else jnp.float32)
            for offset in owner_offsets
        ],
        in_specs=[vmem] * len(operands),
        out_specs=[vmem] * far,
        compiler_params=params,
    )(*held(pltpu.VMEM, operands))
    parts = [partials[0]]
    for offset in far_offsets[-1:] + far_offsets[1:-1]:
        parts.append(swap(partials[owner_offsets.index(offset)], offset))
    return pl.pallas_call(
        merge_kernel,
        out_shape=jax.ShapeDtypeStruct((local_rows, WIDTH), jnp.bfloat16),
        in_specs=[vmem] * far,
        out_specs=vmem,
        compiler_params=params,
    )(*held(pltpu.VMEM, parts))


def solution(mesh):
    placed = (
        P(("group", "rows"), None),
        P(("group", "rows"), None),
        P(("group", "rows"), None),
        P(("group", "rows"), None),
        P(("group", "rows"), None),
        P("group"),
    )
    return jax.shard_map(
        shards, mesh=mesh, in_specs=placed, out_specs=P(("group", "rows"), None), check_vma=False
    )
```

```python
import functools

import jax
import jax.numpy as jnp
from jax import lax
from jax.experimental import pallas as pl
from jax.experimental.pallas import tpu as pltpu
from jax.sharding import PartitionSpec as P

QUERY_HEADS = 24
KV_HEADS = 8
HEAD_DIM = 128
TREE_DEPTH = 4
GROUPS = QUERY_HEADS // KV_HEADS
WIDTH = QUERY_HEADS * HEAD_DIM
LANES = 128
STRIDE = 32
CHUNKS = 4
NT = (((1,), (1,)), ((), ()))
SCHEDULE_LAST = pl.CostEstimate(flops=3 * 10**10, bytes_accessed=10**8, transcendentals=0)
HEADS = [slice(head * HEAD_DIM, (head + 1) * HEAD_DIM) for head in range(QUERY_HEADS)]


def rest_kernel(prefix_values, tree_keys, tree_values, rest, tree_scratch, sems):
    slab = prefix_values.shape[0]
    chunk = slab // CHUNKS
    copies = [
        pltpu.make_async_copy(tree_keys, tree_scratch.at[0], sems.at[0]),
        pltpu.make_async_copy(tree_values, tree_scratch.at[1], sems.at[1]),
    ]
    for place in range(CHUNKS):
        rows = slice(place * chunk, (place + 1) * chunk)
        copies.append(pltpu.make_async_copy(prefix_values.at[rows], rest.at[rows], sems.at[2 + place]))
    for copy in copies:
        copy.start()
    for copy in copies:
        copy.wait()
    trees = [tree_scratch[0].astype(jnp.float32), tree_scratch[1].astype(jnp.float32)]
    local_rows = (rest.shape[0] - slab) // 2
    for head in range(KV_HEADS):
        rows = slice(head * local_rows, (head + 1) * local_rows)
        both = jnp.concatenate([tree[rows] for tree in trees], axis=0)
        rest[slab:, HEADS[head]] = both.astype(rest.dtype)


def stack_kernel(*refs):
    blocks, out = refs[:-1], refs[-1]
    first = 0
    for block in blocks:
        out[first : first + block.shape[0]] = block[...]
        first += block.shape[0]


def chosen(index, values):
    picked = jnp.full(index.shape, values[0], jnp.int32)
    for place in range(1, len(values)):
        picked = jnp.where(index == place, values[place], picked)
    return picked


def mask_kernel(owner_offsets, token_offsets, local_rows, parents, bias):
    position = lax.axis_index("rows")
    rows, columns = bias.shape
    block = columns // len(token_offsets)
    slab = block - 2 * local_rows
    slot = lax.broadcasted_iota(jnp.int32, (rows, 1), 0)
    walker = (position ^ chosen(slot // local_rows, owner_offsets)) * local_rows + slot % local_rows
    slot = lax.broadcasted_iota(jnp.int32, (1, columns), 1)
    within = slot % block - slab
    token = (position ^ chosen(slot // block, token_offsets)) * local_rows + within
    is_tree = (within >= 0) & (within < local_rows)
    candidates = lax.broadcasted_iota(jnp.int32, (rows, parents.shape[1]), 1)
    parent = parents[...]
    allowed = walker == token
    for _ in range(TREE_DEPTH - 1):
        walker = jnp.sum(jnp.where(walker == candidates, parent, 0), axis=1, keepdims=True)
        allowed = allowed | (walker == token)
    bias[...] = jnp.where((allowed & is_tree) | (within < 0), 0.0, -jnp.inf)


def block_rows(parts, local_rows):
    keys, values = [], []
    for slab_keys, rest in parts:
        slab = slab_keys.shape[0]
        tree = rest[slab:]
        halves = tree.astype(jnp.float32)
        turned = jnp.concatenate([halves[local_rows:], halves[:local_rows]], axis=0)
        keys += [slab_keys[...], tree]
        values += [rest[:slab], turned.astype(jnp.bfloat16)]
    return keys, values


def bundle_parts(bundle, last_rest, count, slab, local_rows):
    block = slab + 2 * local_rows
    rests = [bundle.at[count * slab + i * block : count * slab + (i + 1) * block] for i in range(count - 1)]
    return [(bundle.at[i * slab : (i + 1) * slab], rest) for i, rest in enumerate(rests + [last_rest])]


def rows_kernel(*refs):
    blocks, out = refs[:-1], refs[-1]
    rows = blocks[0].shape[0]
    for place in range(0, len(blocks), 2):
        both = [block[...].astype(jnp.float32) for block in blocks[place : place + 2]]
        out[place * rows : (place + 2) * rows] = jnp.concatenate(both, axis=0).astype(out.dtype)


def attend_kernel(owners, count, slab, queries, near_bundle, near_rest, far_bundle, far_rest, bias_ref, *outs):
    rows = queries.shape[0]
    local_rows = rows // owners
    parts = bundle_parts(near_bundle, near_rest, count, slab, local_rows)
    parts += bundle_parts(far_bundle, far_rest, count, slab, local_rows)
    key_parts, value_parts = block_rows(parts, local_rows)
    bias = jnp.concatenate([bias_ref[...]] * GROUPS, axis=0)
    scores = []
    for head in range(KV_HEADS):
        query = jnp.concatenate([queries[:, HEADS[head * GROUPS + g]] for g in range(GROUPS)], axis=0)
        keys = jnp.concatenate([part[:, HEADS[head]] for part in key_parts], axis=0)
        products = lax.dot_general(query, keys, NT, preferred_element_type=jnp.float32)
        scores.append(products * HEAD_DIM ** (-0.5) + bias)
    weights = []
    for head in range(KV_HEADS):
        maxima = jnp.max(scores[head], axis=1, keepdims=True)
        exps = jnp.exp(scores[head] - maxima)
        masses = jnp.sum(exps, axis=1, keepdims=True)
        weights.append((exps.astype(jnp.bfloat16), maxima + jnp.log(masses), 1.0 / masses))
    lane = lax.broadcasted_iota(jnp.int32, (rows, LANES), 1)
    stats = jnp.zeros((rows, LANES), jnp.float32)
    for head, (rounded, level, inverse) in enumerate(weights):
        values = jnp.concatenate([part[:, HEADS[head]] for part in value_parts], axis=0)
        weighted = jnp.dot(rounded, values, preferred_element_type=jnp.float32) * inverse
        for g in range(GROUPS):
            query_head = head * GROUPS + g
            here = (lane % STRIDE == query_head) & (lane < 3 * STRIDE)
            stats = jnp.where(here, level[g * rows : (g + 1) * rows], stats)
            for owner in range(owners):
                first = g * rows + owner * local_rows
                outs[owner][:, HEADS[query_head]] = weighted[first : first + local_rows].astype(outs[owner].dtype)
    high = stats.astype(jnp.bfloat16).astype(jnp.float32)
    left = stats - high
    middle = left.astype(jnp.bfloat16).astype(jnp.float32)
    low = left - middle
    sent = jnp.where(lane < STRIDE, high, jnp.where(lane < 2 * STRIDE, middle, low))
    for owner in range(owners):
        outs[owner][:, WIDTH:] = sent[owner * local_rows : (owner + 1) * local_rows].astype(outs[owner].dtype)


def merge_kernel(*refs):
    parts, out = refs[:-1], refs[-1]
    levels = []
    for part in parts:
        terms = part[:, WIDTH:].astype(jnp.float32)
        levels.append(terms + pltpu.roll(terms, LANES - STRIDE, 1) + pltpu.roll(terms, LANES - 2 * STRIDE, 1))
    top = functools.reduce(jnp.maximum, levels)
    shares = [jnp.exp(level - top) for level in levels]
    whole = 1.0 / functools.reduce(jnp.add, shares)
    shares = [share * whole for share in shares]
    for head in range(QUERY_HEADS):
        total = functools.reduce(
            jnp.add,
            [
                share[:, head : head + 1] * part[:, HEADS[head]].astype(jnp.float32)
                for share, part in zip(shares, parts)
            ],
        )
        out[:, HEADS[head]] = total.astype(out.dtype)


def held(memory, arrays):
    return [pltpu.with_memory_space_constraint(x, memory) for x in arrays]


def swap(x, offset):
    return lax.ppermute(x, "rows", [(i, i ^ offset) for i in range(lax.axis_size("rows"))])


def by_head(x):
    return jnp.transpose(x.reshape(-1, KV_HEADS, HEAD_DIM), (1, 0, 2)).reshape(-1, HEAD_DIM)


def after(x, *earlier):
    return lax.optimization_barrier((x, *earlier))


def shards(queries, prefix_keys, prefix_values, tree_keys, tree_values, parents):
    size = lax.axis_size("rows")
    bits = size.bit_length() - 1
    near_bits = (bits + 1) // 2
    near = 2**near_bits
    far = size // near
    local_rows = queries.shape[0]
    slab, row_width = prefix_keys.shape
    far_offsets = [0] + [near * i | 1 for i in range(1, far)]
    far_order = far_offsets[2:] + far_offsets[1:2]
    vmem = pl.BlockSpec(memory_space=pltpu.VMEM)
    hbm = pl.BlockSpec(memory_space=pltpu.HBM)
    params = pltpu.CompilerParams(vmem_limit_bytes=16 * 2**20)
    own_rest = pl.pallas_call(
        rest_kernel,
        out_shape=pltpu.VMEM((slab + 2 * local_rows, row_width), prefix_values.dtype),
        in_specs=[hbm] * 3,
        out_specs=vmem,
        scratch_shapes=[
            pltpu.VMEM((2, KV_HEADS * local_rows, HEAD_DIM), tree_keys.dtype),
            pltpu.SemaphoreType.DMA((2 + CHUNKS,)),
        ],
        compiler_params=params,
    )(*held(pltpu.HBM, [prefix_values, by_head(tree_keys), by_head(tree_values)]))

    owner_offsets = [0] + far_order
    key_pieces, rest_pieces = {0: prefix_keys}, {0: own_rest}
    for bit in reversed(range(1, near_bits)):
        for offset in list(key_pieces):
            step = 1 << bit
            key_pieces[offset ^ step] = swap(key_pieces[offset], step)
            rest_pieces[offset ^ step] = swap(rest_pieces[offset], step)
    block_offsets = list(key_pieces)
    sibling_offsets = [offset ^ 1 for offset in block_offsets]
    mask = pl.pallas_call(
        functools.partial(mask_kernel, owner_offsets, block_offsets + sibling_offsets, local_rows),
        out_shape=pltpu.VMEM((far * local_rows, near * (slab + 2 * local_rows)), jnp.float32),
        in_specs=[vmem],
        out_specs=vmem,
        compiler_params=params,
    )(parents[None, :])
    all_queries = {0: queries}
    for offset in far_order:
        sent = queries
        if offset == far_order[-1]:
            sent, key_pieces[block_offsets[-1]] = after(sent, key_pieces[block_offsets[-1]])
        all_queries[offset] = swap(sent, offset)
    gathered = pl.pallas_call(
        rows_kernel,
        out_shape=pltpu.VMEM((far * local_rows, WIDTH), queries.dtype),
        in_specs=[vmem] * far,
        out_specs=vmem,
        compiler_params=params,
        cost_estimate=SCHEDULE_LAST,
    )(*held(pltpu.VMEM, [all_queries[offset] for offset in owner_offsets]))
    blocks = list(key_pieces.values()) + list(rest_pieces.values())[:-1]
    bundle = pl.pallas_call(
        stack_kernel,
        out_shape=pltpu.VMEM((sum(block.shape[0] for block in blocks), row_width), prefix_keys.dtype),
        in_specs=[vmem] * len(blocks),
        out_specs=vmem,
        compiler_params=params,
    )(*held(pltpu.VMEM, blocks))
    last_rest = list(rest_pieces.values())[-1]
    far_bundle, far_rest = swap(bundle, 1), swap(last_rest, 1)
    count = len(block_offsets)
    operands = [gathered, bundle, last_rest, far_bundle, far_rest, mask]
    partials = pl.pallas_call(
        functools.partial(attend_kernel, far, count, slab),
        out_shape=[
            pltpu.VMEM((local_rows, WIDTH + LANES), jnp.bfloat16 if offset else jnp.float32)
            for offset in owner_offsets
        ],
        in_specs=[vmem] * len(operands),
        out_specs=[vmem] * far,
        compiler_params=params,
    )(*held(pltpu.VMEM, operands))
    parts = [partials[0]]
    for offset in far_offsets[-1:] + far_offsets[1:-1]:
        parts.append(swap(partials[owner_offsets.index(offset)], offset))
    return pl.pallas_call(
        merge_kernel,
        out_shape=jax.ShapeDtypeStruct((local_rows, WIDTH), jnp.bfloat16),
        in_specs=[vmem] * far,
        out_specs=vmem,
        compiler_params=params,
    )(*held(pltpu.VMEM, parts))


def solution(mesh):
    placed = (
        P(("group", "rows"), None),
        P(("group", "rows"), None),
        P(("group", "rows"), None),
        P(("group", "rows"), None),
        P(("group", "rows"), None),
        P("group"),
    )
    return jax.shard_map(
        shards, mesh=mesh, in_specs=placed, out_specs=P(("group", "rows"), None), check_vma=False
    )
```

```python
import functools

import jax
import jax.numpy as jnp
from jax import lax
from jax.experimental import pallas as pl
from jax.experimental.pallas import tpu as pltpu
from jax.sharding import PartitionSpec as P

QUERY_HEADS = 24
KV_HEADS = 8
HEAD_DIM = 128
TREE_DEPTH = 4
GROUPS = QUERY_HEADS // KV_HEADS
WIDTH = QUERY_HEADS * HEAD_DIM
LANES = 128
STRIDE = 32
CHUNKS = 4
NT = (((1,), (1,)), ((), ()))
LOG2_E = 1.4426950408889634
SCHEDULE_LAST = pl.CostEstimate(flops=3 * 10**10, bytes_accessed=10**8, transcendentals=0)
HEADS = [slice(head * HEAD_DIM, (head + 1) * HEAD_DIM) for head in range(QUERY_HEADS)]


def rest_kernel(prefix_values, tree_keys, tree_values, rest, tree_scratch, sems):
    slab = prefix_values.shape[0]
    chunk = slab // CHUNKS
    copies = [
        pltpu.make_async_copy(tree_keys, tree_scratch.at[0], sems.at[0]),
        pltpu.make_async_copy(tree_values, tree_scratch.at[1], sems.at[1]),
    ]
    for place in range(CHUNKS):
        rows = slice(place * chunk, (place + 1) * chunk)
        copies.append(pltpu.make_async_copy(prefix_values.at[rows], rest.at[rows], sems.at[2 + place]))
    for copy in copies:
        copy.start()
    for copy in copies:
        copy.wait()
    trees = [tree_scratch[0].astype(jnp.float32), tree_scratch[1].astype(jnp.float32)]
    local_rows = (rest.shape[0] - slab) // 2
    for head in range(KV_HEADS):
        rows = slice(head * local_rows, (head + 1) * local_rows)
        both = jnp.concatenate([tree[rows] for tree in trees], axis=0)
        rest[slab:, HEADS[head]] = both.astype(rest.dtype)


def stack_kernel(*refs):
    blocks, out = refs[:-1], refs[-1]
    first = 0
    for block in blocks:
        out[first : first + block.shape[0]] = block[...]
        first += block.shape[0]


def chosen(index, values):
    picked = jnp.full(index.shape, values[0], jnp.int32)
    for place in range(1, len(values)):
        picked = jnp.where(index == place, values[place], picked)
    return picked


def mask_kernel(owner_offsets, token_offsets, local_rows, parents, bias):
    position = lax.axis_index("rows")
    rows, columns = bias.shape
    block = columns // len(token_offsets)
    slab = block - 2 * local_rows
    slot = lax.broadcasted_iota(jnp.int32, (rows, 1), 0)
    walker = (position ^ chosen(slot // local_rows, owner_offsets)) * local_rows + slot % local_rows
    slot = lax.broadcasted_iota(jnp.int32, (1, columns), 1)
    within = slot % block - slab
    token = (position ^ chosen(slot // block, token_offsets)) * local_rows + within
    is_tree = (within >= 0) & (within < local_rows)
    candidates = lax.broadcasted_iota(jnp.int32, (rows, parents.shape[1]), 1)
    parent = parents[...]
    allowed = walker == token
    for _ in range(TREE_DEPTH - 1):
        walker = jnp.sum(jnp.where(walker == candidates, parent, 0), axis=1, keepdims=True)
        allowed = allowed | (walker == token)
    bias[...] = jnp.where((allowed & is_tree) | (within < 0), 0.0, -jnp.inf)


def block_rows(parts, local_rows):
    keys, values = [], []
    for slab_keys, rest in parts:
        slab = slab_keys.shape[0]
        tree = rest[slab:]
        halves = tree.astype(jnp.float32)
        turned = jnp.concatenate([halves[local_rows:], halves[:local_rows]], axis=0)
        keys += [slab_keys[...], tree]
        values += [rest[:slab], turned.astype(jnp.bfloat16)]
    return keys, values


def bundle_parts(bundle, last_rest, count, slab, local_rows):
    block = slab + 2 * local_rows
    rests = [bundle.at[count * slab + i * block : count * slab + (i + 1) * block] for i in range(count - 1)]
    return [(bundle.at[i * slab : (i + 1) * slab], rest) for i, rest in enumerate(rests + [last_rest])]


def rows_kernel(*refs):
    blocks, out = refs[:-1], refs[-1]
    rows = blocks[0].shape[0]
    for place in range(0, len(blocks), 2):
        both = [block[...].astype(jnp.float32) for block in blocks[place : place + 2]]
        out[place * rows : (place + 2) * rows] = jnp.concatenate(both, axis=0).astype(out.dtype)


def attend_kernel(owners, count, slab, queries, near_bundle, near_rest, far_bundle, far_rest, bias_ref, *outs):
    rows = queries.shape[0]
    local_rows = rows // owners
    parts = bundle_parts(near_bundle, near_rest, count, slab, local_rows)
    parts += bundle_parts(far_bundle, far_rest, count, slab, local_rows)
    key_parts, value_parts = block_rows(parts, local_rows)
    bias = jnp.concatenate([bias_ref[...]] * GROUPS, axis=0)
    scores = []
    for head in range(KV_HEADS):
        query = jnp.concatenate([queries[:, HEADS[head * GROUPS + g]] for g in range(GROUPS)], axis=0)
        keys = jnp.concatenate([part[:, HEADS[head]] for part in key_parts], axis=0)
        products = lax.dot_general(query, keys, NT, preferred_element_type=jnp.float32)
        scores.append(products * (HEAD_DIM ** (-0.5) * LOG2_E) + bias)
    weights = []
    for head in range(KV_HEADS):
        maxima = jnp.max(scores[head], axis=1, keepdims=True)
        exps = jnp.exp2(scores[head] - maxima)
        masses = jnp.sum(exps, axis=1, keepdims=True)
        weights.append((exps.astype(jnp.bfloat16), maxima + jnp.log2(masses), 1.0 / masses))
    lane = lax.broadcasted_iota(jnp.int32, (rows, LANES), 1)
    stats = jnp.zeros((rows, LANES), jnp.float32)
    for head, (rounded, level, inverse) in enumerate(weights):
        values = jnp.concatenate([part[:, HEADS[head]] for part in value_parts], axis=0)
        weighted = jnp.dot(rounded, values, preferred_element_type=jnp.float32) * inverse
        for g in range(GROUPS):
            query_head = head * GROUPS + g
            here = (lane % STRIDE == query_head) & (lane < 3 * STRIDE)
            stats = jnp.where(here, level[g * rows : (g + 1) * rows], stats)
            for owner in range(owners):
                first = g * rows + owner * local_rows
                outs[owner][:, HEADS[query_head]] = weighted[first : first + local_rows].astype(outs[owner].dtype)
    high = stats.astype(jnp.bfloat16).astype(jnp.float32)
    left = stats - high
    middle = left.astype(jnp.bfloat16).astype(jnp.float32)
    low = left - middle
    sent = jnp.where(lane < STRIDE, high, jnp.where(lane < 2 * STRIDE, middle, low))
    for owner in range(owners):
        outs[owner][:, WIDTH:] = sent[owner * local_rows : (owner + 1) * local_rows].astype(outs[owner].dtype)


def merge_kernel(*refs):
    parts, out = refs[:-1], refs[-1]
    levels = []
    for part in parts:
        terms = part[:, WIDTH:].astype(jnp.float32)
        levels.append(terms + pltpu.roll(terms, LANES - STRIDE, 1) + pltpu.roll(terms, LANES - 2 * STRIDE, 1))
    top = functools.reduce(jnp.maximum, levels)
    shares = [jnp.exp2(level - top) for level in levels]
    whole = 1.0 / functools.reduce(jnp.add, shares)
    shares = [share * whole for share in shares]
    for head in range(QUERY_HEADS):
        total = functools.reduce(
            jnp.add,
            [
                share[:, head : head + 1] * part[:, HEADS[head]].astype(jnp.float32)
                for share, part in zip(shares, parts)
            ],
        )
        out[:, HEADS[head]] = total.astype(out.dtype)


def held(memory, arrays):
    return [pltpu.with_memory_space_constraint(x, memory) for x in arrays]


def swap(x, offset):
    return lax.ppermute(x, "rows", [(i, i ^ offset) for i in range(lax.axis_size("rows"))])


def by_head(x):
    return jnp.transpose(x.reshape(-1, KV_HEADS, HEAD_DIM), (1, 0, 2)).reshape(-1, HEAD_DIM)


def after(x, *earlier):
    return lax.optimization_barrier((x, *earlier))


def shards(queries, prefix_keys, prefix_values, tree_keys, tree_values, parents):
    size = lax.axis_size("rows")
    bits = size.bit_length() - 1
    near_bits = (bits + 1) // 2
    near = 2**near_bits
    far = size // near
    local_rows = queries.shape[0]
    slab, row_width = prefix_keys.shape
    far_offsets = [0] + [near * i | 1 for i in range(1, far)]
    far_order = far_offsets[2:] + far_offsets[1:2]
    vmem = pl.BlockSpec(memory_space=pltpu.VMEM)
    hbm = pl.BlockSpec(memory_space=pltpu.HBM)
    params = pltpu.CompilerParams(vmem_limit_bytes=16 * 2**20)
    own_rest = pl.pallas_call(
        rest_kernel,
        out_shape=pltpu.VMEM((slab + 2 * local_rows, row_width), prefix_values.dtype),
        in_specs=[hbm] * 3,
        out_specs=vmem,
        scratch_shapes=[
            pltpu.VMEM((2, KV_HEADS * local_rows, HEAD_DIM), tree_keys.dtype),
            pltpu.SemaphoreType.DMA((2 + CHUNKS,)),
        ],
        compiler_params=params,
    )(*held(pltpu.HBM, [prefix_values, by_head(tree_keys), by_head(tree_values)]))

    owner_offsets = [0] + far_order
    key_pieces, rest_pieces = {0: prefix_keys}, {0: own_rest}
    for bit in reversed(range(1, near_bits)):
        for offset in list(key_pieces):
            step = 1 << bit
            key_pieces[offset ^ step] = swap(key_pieces[offset], step)
            rest_pieces[offset ^ step] = swap(rest_pieces[offset], step)
    block_offsets = list(key_pieces)
    sibling_offsets = [offset ^ 1 for offset in block_offsets]
    mask = pl.pallas_call(
        functools.partial(mask_kernel, owner_offsets, block_offsets + sibling_offsets, local_rows),
        out_shape=pltpu.VMEM((far * local_rows, near * (slab + 2 * local_rows)), jnp.float32),
        in_specs=[vmem],
        out_specs=vmem,
        compiler_params=params,
    )(parents[None, :])
    all_queries = {0: queries}
    for offset in far_order:
        sent = queries
        if offset == far_order[-1]:
            sent, key_pieces[block_offsets[-1]] = after(sent, key_pieces[block_offsets[-1]])
        all_queries[offset] = swap(sent, offset)
    gathered = pl.pallas_call(
        rows_kernel,
        out_shape=pltpu.VMEM((far * local_rows, WIDTH), queries.dtype),
        in_specs=[vmem] * far,
        out_specs=vmem,
        compiler_params=params,
        cost_estimate=SCHEDULE_LAST,
    )(*held(pltpu.VMEM, [all_queries[offset] for offset in owner_offsets]))
    blocks = list(key_pieces.values()) + list(rest_pieces.values())[:-1]
    bundle = pl.pallas_call(
        stack_kernel,
        out_shape=pltpu.VMEM((sum(block.shape[0] for block in blocks), row_width), prefix_keys.dtype),
        in_specs=[vmem] * len(blocks),
        out_specs=vmem,
        compiler_params=params,
    )(*held(pltpu.VMEM, blocks))
    last_rest = list(rest_pieces.values())[-1]
    far_bundle, far_rest = swap(bundle, 1), swap(last_rest, 1)
    count = len(block_offsets)
    operands = [gathered, bundle, last_rest, far_bundle, far_rest, mask]
    partials = pl.pallas_call(
        functools.partial(attend_kernel, far, count, slab),
        out_shape=[
            pltpu.VMEM((local_rows, WIDTH + LANES), jnp.bfloat16 if offset else jnp.float32)
            for offset in owner_offsets
        ],
        in_specs=[vmem] * len(operands),
        out_specs=[vmem] * far,
        compiler_params=params,
    )(*held(pltpu.VMEM, operands))
    parts = [partials[0]]
    for offset in far_offsets[-1:] + far_offsets[1:-1]:
        parts.append(swap(partials[owner_offsets.index(offset)], offset))
    return pl.pallas_call(
        merge_kernel,
        out_shape=jax.ShapeDtypeStruct((local_rows, WIDTH), jnp.bfloat16),
        in_specs=[vmem] * far,
        out_specs=vmem,
        compiler_params=params,
    )(*held(pltpu.VMEM, parts))


def solution(mesh):
    placed = (
        P(("group", "rows"), None),
        P(("group", "rows"), None),
        P(("group", "rows"), None),
        P(("group", "rows"), None),
        P(("group", "rows"), None),
        P("group"),
    )
    return jax.shard_map(
        shards, mesh=mesh, in_specs=placed, out_specs=P(("group", "rows"), None), check_vma=False
    )
```

```python
import functools

import jax
import jax.numpy as jnp
from jax import lax
from jax.experimental import pallas as pl
from jax.experimental.pallas import tpu as pltpu
from jax.sharding import PartitionSpec as P

QUERY_HEADS = 24
KV_HEADS = 8
HEAD_DIM = 128
TREE_DEPTH = 4
GROUPS = QUERY_HEADS // KV_HEADS
WIDTH = QUERY_HEADS * HEAD_DIM
LANES = 128
STRIDE = 32
CHUNKS = 4
NT = (((1,), (1,)), ((), ()))
LOG2_E = 1.4426950408889634
SCHEDULE_LAST = pl.CostEstimate(flops=3 * 10**10, bytes_accessed=10**8, transcendentals=0)
HEADS = [slice(head * HEAD_DIM, (head + 1) * HEAD_DIM) for head in range(QUERY_HEADS)]


def rest_kernel(prefix_values, tree_keys, tree_values, rest, tree_scratch, sems):
    slab = prefix_values.shape[0]
    chunk = slab // CHUNKS
    copies = [
        pltpu.make_async_copy(tree_keys, tree_scratch.at[0], sems.at[0]),
        pltpu.make_async_copy(tree_values, tree_scratch.at[1], sems.at[1]),
    ]
    for place in range(CHUNKS):
        rows = slice(place * chunk, (place + 1) * chunk)
        copies.append(pltpu.make_async_copy(prefix_values.at[rows], rest.at[rows], sems.at[2 + place]))
    for copy in copies:
        copy.start()
    for copy in copies:
        copy.wait()
    trees = [tree_scratch[0].astype(jnp.float32), tree_scratch[1].astype(jnp.float32)]
    local_rows = (rest.shape[0] - slab) // 2
    for head in range(KV_HEADS):
        rows = slice(head * local_rows, (head + 1) * local_rows)
        both = jnp.concatenate([tree[rows] for tree in trees], axis=0)
        rest[slab:, HEADS[head]] = both.astype(rest.dtype)


def stack_kernel(*refs):
    blocks, out = refs[:-1], refs[-1]
    first = 0
    for block in blocks:
        out[first : first + block.shape[0]] = block[...]
        first += block.shape[0]


def chosen(index, values):
    picked = jnp.full(index.shape, values[0], jnp.int32)
    for place in range(1, len(values)):
        picked = jnp.where(index == place, values[place], picked)
    return picked


def mask_kernel(owner_offsets, token_offsets, local_rows, parents, bias):
    position = lax.axis_index("rows")
    rows, columns = bias.shape
    block = columns // len(token_offsets)
    slab = block - 2 * local_rows
    slot = lax.broadcasted_iota(jnp.int32, (rows, 1), 0)
    walker = (position ^ chosen(slot // local_rows, owner_offsets)) * local_rows + slot % local_rows
    slot = lax.broadcasted_iota(jnp.int32, (1, columns), 1)
    within = slot % block - slab
    token = (position ^ chosen(slot // block, token_offsets)) * local_rows + within
    is_tree = (within >= 0) & (within < local_rows)
    candidates = lax.broadcasted_iota(jnp.int32, (rows, parents.shape[1]), 1)
    parent = parents[...]
    allowed = walker == token
    for _ in range(TREE_DEPTH - 1):
        walker = jnp.sum(jnp.where(walker == candidates, parent, 0), axis=1, keepdims=True)
        allowed = allowed | (walker == token)
    bias[...] = jnp.where((allowed & is_tree) | (within < 0), 0.0, -jnp.inf)


def block_rows(parts, local_rows):
    keys, values = [], []
    for slab_keys, rest in parts:
        slab = slab_keys.shape[0]
        tree = rest[slab:]
        halves = tree.astype(jnp.float32)
        turned = jnp.concatenate([halves[local_rows:], halves[:local_rows]], axis=0)
        keys += [slab_keys[...], tree]
        values += [rest[:slab], turned.astype(jnp.bfloat16)]
    return keys, values


def bundle_parts(bundle, last_rest, count, slab, local_rows):
    block = slab + 2 * local_rows
    rests = [bundle.at[count * slab + i * block : count * slab + (i + 1) * block] for i in range(count - 1)]
    return [(bundle.at[i * slab : (i + 1) * slab], rest) for i, rest in enumerate(rests + [last_rest])]


def rows_kernel(*refs):
    blocks, out = refs[:-1], refs[-1]
    rows = blocks[0].shape[0]
    for place in range(0, len(blocks), 2):
        both = [block[...].astype(jnp.float32) for block in blocks[place : place + 2]]
        out[place * rows : (place + 2) * rows] = jnp.concatenate(both, axis=0).astype(out.dtype)


def attend_kernel(owners, count, slab, queries, near_bundle, near_rest, far_bundle, far_rest, bias_ref, *outs):
    rows = queries.shape[0]
    local_rows = rows // owners
    parts = bundle_parts(near_bundle, near_rest, count, slab, local_rows)
    parts += bundle_parts(far_bundle, far_rest, count, slab, local_rows)
    key_parts, value_parts = block_rows(parts, local_rows)
    bias = jnp.concatenate([bias_ref[...]] * GROUPS, axis=0)
    scores = []
    for head in range(KV_HEADS):
        query = jnp.concatenate([queries[:, HEADS[head * GROUPS + g]] for g in range(GROUPS)], axis=0)
        keys = jnp.concatenate([part[:, HEADS[head]] for part in key_parts], axis=0)
        products = lax.dot_general(query, keys, NT, preferred_element_type=jnp.float32)
        scores.append(products * (HEAD_DIM ** (-0.5) * LOG2_E) + bias)
    weights = []
    for head in range(KV_HEADS):
        maxima = jnp.max(scores[head], axis=1, keepdims=True)
        exps = jnp.exp2(scores[head] - maxima)
        masses = jnp.sum(exps, axis=1, keepdims=True)
        weights.append((exps.astype(jnp.bfloat16), maxima + jnp.log2(masses), 1.0 / masses))
    lane = lax.broadcasted_iota(jnp.int32, (rows, LANES), 1)
    stats = jnp.zeros((rows, LANES), jnp.float32)
    for head, (rounded, level, inverse) in enumerate(weights):
        values = jnp.concatenate([part[:, HEADS[head]] for part in value_parts], axis=0)
        weighted = jnp.dot(rounded, values, preferred_element_type=jnp.float32) * inverse
        for g in range(GROUPS):
            query_head = head * GROUPS + g
            here = (lane % STRIDE == query_head) & (lane < 3 * STRIDE)
            stats = jnp.where(here, level[g * rows : (g + 1) * rows], stats)
            for owner in range(owners):
                first = g * rows + owner * local_rows
                outs[owner][:, HEADS[query_head]] = weighted[first : first + local_rows].astype(outs[owner].dtype)
    high = stats.astype(jnp.bfloat16).astype(jnp.float32)
    left = stats - high
    middle = left.astype(jnp.bfloat16).astype(jnp.float32)
    low = left - middle
    sent = jnp.where(lane < STRIDE, high, jnp.where(lane < 2 * STRIDE, middle, low))
    for owner in range(owners):
        outs[owner][:, WIDTH:] = sent[owner * local_rows : (owner + 1) * local_rows].astype(outs[owner].dtype)


def merge_kernel(*refs):
    parts, out = refs[:-1], refs[-1]
    levels = []
    for part in parts:
        terms = part[:, WIDTH:].astype(jnp.float32)
        levels.append(terms + pltpu.roll(terms, LANES - STRIDE, 1) + pltpu.roll(terms, LANES - 2 * STRIDE, 1))
    top = functools.reduce(jnp.maximum, levels)
    shares = [jnp.exp2(level - top) for level in levels]
    whole = 1.0 / functools.reduce(jnp.add, shares)
    shares = [share * whole for share in shares]
    for head in range(QUERY_HEADS):
        own = parts[0][:, HEADS[head]]
        total = own
        for share, part in zip(shares[1:], parts[1:]):
            total = total + share[:, head : head + 1] * (part[:, HEADS[head]].astype(jnp.float32) - own)
        out[:, HEADS[head]] = total.astype(out.dtype)


def held(memory, arrays):
    return [pltpu.with_memory_space_constraint(x, memory) for x in arrays]


def swap(x, offset):
    return lax.ppermute(x, "rows", [(i, i ^ offset) for i in range(lax.axis_size("rows"))])


def by_head(x):
    return jnp.transpose(x.reshape(-1, KV_HEADS, HEAD_DIM), (1, 0, 2)).reshape(-1, HEAD_DIM)


def after(x, *earlier):
    return lax.optimization_barrier((x, *earlier))


def shards(queries, prefix_keys, prefix_values, tree_keys, tree_values, parents):
    size = lax.axis_size("rows")
    bits = size.bit_length() - 1
    near_bits = (bits + 1) // 2
    near = 2**near_bits
    far = size // near
    local_rows = queries.shape[0]
    slab, row_width = prefix_keys.shape
    far_offsets = [0] + [near * i | 1 for i in range(1, far)]
    far_order = far_offsets[2:] + far_offsets[1:2]
    vmem = pl.BlockSpec(memory_space=pltpu.VMEM)
    hbm = pl.BlockSpec(memory_space=pltpu.HBM)
    params = pltpu.CompilerParams(vmem_limit_bytes=16 * 2**20)
    own_rest = pl.pallas_call(
        rest_kernel,
        out_shape=pltpu.VMEM((slab + 2 * local_rows, row_width), prefix_values.dtype),
        in_specs=[hbm] * 3,
        out_specs=vmem,
        scratch_shapes=[
            pltpu.VMEM((2, KV_HEADS * local_rows, HEAD_DIM), tree_keys.dtype),
            pltpu.SemaphoreType.DMA((2 + CHUNKS,)),
        ],
        compiler_params=params,
    )(*held(pltpu.HBM, [prefix_values, by_head(tree_keys), by_head(tree_values)]))

    owner_offsets = [0] + far_order
    key_pieces, rest_pieces = {0: prefix_keys}, {0: own_rest}
    for bit in reversed(range(1, near_bits)):
        for offset in list(key_pieces):
            step = 1 << bit
            key_pieces[offset ^ step] = swap(key_pieces[offset], step)
            rest_pieces[offset ^ step] = swap(rest_pieces[offset], step)
    block_offsets = list(key_pieces)
    sibling_offsets = [offset ^ 1 for offset in block_offsets]
    mask = pl.pallas_call(
        functools.partial(mask_kernel, owner_offsets, block_offsets + sibling_offsets, local_rows),
        out_shape=pltpu.VMEM((far * local_rows, near * (slab + 2 * local_rows)), jnp.float32),
        in_specs=[vmem],
        out_specs=vmem,
        compiler_params=params,
    )(parents[None, :])
    all_queries = {0: queries}
    for offset in far_order:
        sent = queries
        if offset == far_order[-1]:
            sent, key_pieces[block_offsets[-1]] = after(sent, key_pieces[block_offsets[-1]])
        all_queries[offset] = swap(sent, offset)
    gathered = pl.pallas_call(
        rows_kernel,
        out_shape=pltpu.VMEM((far * local_rows, WIDTH), queries.dtype),
        in_specs=[vmem] * far,
        out_specs=vmem,
        compiler_params=params,
        cost_estimate=SCHEDULE_LAST,
    )(*held(pltpu.VMEM, [all_queries[offset] for offset in owner_offsets]))
    blocks = list(key_pieces.values()) + list(rest_pieces.values())[:-1]
    bundle = pl.pallas_call(
        stack_kernel,
        out_shape=pltpu.VMEM((sum(block.shape[0] for block in blocks), row_width), prefix_keys.dtype),
        in_specs=[vmem] * len(blocks),
        out_specs=vmem,
        compiler_params=params,
    )(*held(pltpu.VMEM, blocks))
    last_rest = list(rest_pieces.values())[-1]
    far_bundle, far_rest = swap(bundle, 1), swap(last_rest, 1)
    count = len(block_offsets)
    operands = [gathered, bundle, last_rest, far_bundle, far_rest, mask]
    partials = pl.pallas_call(
        functools.partial(attend_kernel, far, count, slab),
        out_shape=[
            pltpu.VMEM((local_rows, WIDTH + LANES), jnp.bfloat16 if offset else jnp.float32)
            for offset in owner_offsets
        ],
        in_specs=[vmem] * len(operands),
        out_specs=[vmem] * far,
        compiler_params=params,
    )(*held(pltpu.VMEM, operands))
    parts = [partials[0]]
    for offset in far_offsets[-1:] + far_offsets[1:-1]:
        parts.append(swap(partials[owner_offsets.index(offset)], offset))
    return pl.pallas_call(
        merge_kernel,
        out_shape=jax.ShapeDtypeStruct((local_rows, WIDTH), jnp.bfloat16),
        in_specs=[vmem] * far,
        out_specs=vmem,
        compiler_params=params,
    )(*held(pltpu.VMEM, parts))


def solution(mesh):
    placed = (
        P(("group", "rows"), None),
        P(("group", "rows"), None),
        P(("group", "rows"), None),
        P(("group", "rows"), None),
        P(("group", "rows"), None),
        P("group"),
    )
    return jax.shard_map(
        shards, mesh=mesh, in_specs=placed, out_specs=P(("group", "rows"), None), check_vma=False
    )
```

```python
import functools

import jax
import jax.numpy as jnp
from jax import lax
from jax.experimental import pallas as pl
from jax.experimental.pallas import tpu as pltpu
from jax.sharding import PartitionSpec as P

QUERY_HEADS = 24
KV_HEADS = 8
HEAD_DIM = 128
TREE_DEPTH = 4
GROUPS = QUERY_HEADS // KV_HEADS
WIDTH = QUERY_HEADS * HEAD_DIM
LANES = 128
STRIDE = 32
CHUNKS = 4
NT = (((1,), (1,)), ((), ()))
LOG2_E = 1.4426950408889634
SCHEDULE_LAST = pl.CostEstimate(flops=3 * 10**10, bytes_accessed=10**8, transcendentals=0)
HEADS = [slice(head * HEAD_DIM, (head + 1) * HEAD_DIM) for head in range(QUERY_HEADS)]


def rest_kernel(prefix_values, tree_keys, tree_values, rest, tree_scratch, sems):
    slab = prefix_values.shape[0]
    chunk = slab // CHUNKS
    copies = [
        pltpu.make_async_copy(tree_keys, tree_scratch.at[0], sems.at[0]),
        pltpu.make_async_copy(tree_values, tree_scratch.at[1], sems.at[1]),
    ]
    for place in range(CHUNKS):
        rows = slice(place * chunk, (place + 1) * chunk)
        copies.append(pltpu.make_async_copy(prefix_values.at[rows], rest.at[rows], sems.at[2 + place]))
    for copy in copies:
        copy.start()
    for copy in copies:
        copy.wait()
    trees = [tree_scratch[0].astype(jnp.float32), tree_scratch[1].astype(jnp.float32)]
    local_rows = (rest.shape[0] - slab) // 2
    for head in range(KV_HEADS):
        rows = slice(head * local_rows, (head + 1) * local_rows)
        both = jnp.concatenate([tree[rows] for tree in trees], axis=0)
        rest[slab:, HEADS[head]] = both.astype(rest.dtype)


def stack_kernel(*refs):
    blocks, out = refs[:-1], refs[-1]
    first = 0
    for block in blocks:
        out[first : first + block.shape[0]] = block[...]
        first += block.shape[0]


def chosen(index, values):
    picked = jnp.full(index.shape, values[0], jnp.int32)
    for place in range(1, len(values)):
        picked = jnp.where(index == place, values[place], picked)
    return picked


def mask_kernel(owner_offsets, token_offsets, local_rows, parents, bias):
    position = lax.axis_index("rows")
    rows, columns = bias.shape
    block = columns // len(token_offsets)
    slab = block - 2 * local_rows
    slot = lax.broadcasted_iota(jnp.int32, (rows, 1), 0)
    walker = (position ^ chosen(slot // local_rows, owner_offsets)) * local_rows + slot % local_rows
    slot = lax.broadcasted_iota(jnp.int32, (1, columns), 1)
    within = slot % block - slab
    token = (position ^ chosen(slot // block, token_offsets)) * local_rows + within
    is_tree = (within >= 0) & (within < local_rows)
    candidates = lax.broadcasted_iota(jnp.int32, (rows, parents.shape[1]), 1)
    parent = parents[...]
    allowed = walker == token
    for _ in range(TREE_DEPTH - 1):
        walker = jnp.sum(jnp.where(walker == candidates, parent, 0), axis=1, keepdims=True)
        allowed = allowed | (walker == token)
    bias[...] = jnp.where((allowed & is_tree) | (within < 0), 0.0, -jnp.inf)


def block_rows(parts, local_rows):
    keys, values = [], []
    for slab_keys, rest in parts:
        slab = slab_keys.shape[0]
        tree = rest[slab:]
        halves = tree.astype(jnp.float32)
        turned = jnp.concatenate([halves[local_rows:], halves[:local_rows]], axis=0)
        keys += [slab_keys[...], tree]
        values += [rest[:slab], turned.astype(jnp.bfloat16)]
    return keys, values


def bundle_parts(bundle, last_rest, count, slab, local_rows):
    block = slab + 2 * local_rows
    rests = [bundle.at[count * slab + i * block : count * slab + (i + 1) * block] for i in range(count - 1)]
    return [(bundle.at[i * slab : (i + 1) * slab], rest) for i, rest in enumerate(rests + [last_rest])]


def rows_kernel(*refs):
    blocks, out = refs[:-1], refs[-1]
    rows = blocks[0].shape[0]
    for place in range(0, len(blocks), 2):
        both = [block[...].astype(jnp.float32) for block in blocks[place : place + 2]]
        out[place * rows : (place + 2) * rows] = jnp.concatenate(both, axis=0).astype(out.dtype)


def attend_kernel(owners, count, slab, queries, near_bundle, near_rest, far_bundle, far_rest, bias_ref, *outs):
    rows = queries.shape[0]
    local_rows = rows // owners
    parts = bundle_parts(near_bundle, near_rest, count, slab, local_rows)
    parts += bundle_parts(far_bundle, far_rest, count, slab, local_rows)
    key_parts, value_parts = block_rows(parts, local_rows)
    bias = jnp.concatenate([bias_ref[...]] * GROUPS, axis=0)
    scores = []
    for head in range(KV_HEADS):
        query = jnp.concatenate([queries[:, HEADS[head * GROUPS + g]] for g in range(GROUPS)], axis=0)
        keys = jnp.concatenate([part[:, HEADS[head]] for part in key_parts], axis=0)
        products = lax.dot_general(query, keys, NT, preferred_element_type=jnp.float32)
        scores.append(products * (HEAD_DIM ** (-0.5) * LOG2_E) + bias)
    weights = []
    for head in range(KV_HEADS):
        maxima = jnp.max(scores[head], axis=1, keepdims=True)
        exps = jnp.exp2(scores[head] - maxima)
        masses = jnp.sum(exps, axis=1, keepdims=True)
        weights.append((exps.astype(jnp.bfloat16), maxima + jnp.log2(masses), 1.0 / masses))
    lane = lax.broadcasted_iota(jnp.int32, (rows, LANES), 1)
    stats = jnp.zeros((rows, LANES), jnp.float32)
    for head, (rounded, level, inverse) in enumerate(weights):
        values = jnp.concatenate([part[:, HEADS[head]] for part in value_parts], axis=0)
        weighted = jnp.dot(rounded, values, preferred_element_type=jnp.float32) * inverse
        for g in range(GROUPS):
            query_head = head * GROUPS + g
            here = (lane % STRIDE == query_head) & (lane < 3 * STRIDE)
            stats = jnp.where(here, level[g * rows : (g + 1) * rows], stats)
            for owner in range(owners):
                first = g * rows + owner * local_rows
                outs[owner][:, HEADS[query_head]] = weighted[first : first + local_rows].astype(outs[owner].dtype)
    high = stats.astype(jnp.bfloat16).astype(jnp.float32)
    left = stats - high
    middle = left.astype(jnp.bfloat16).astype(jnp.float32)
    low = left - middle
    sent = jnp.where(lane < STRIDE, high, jnp.where(lane < 2 * STRIDE, middle, low))
    for owner in range(owners):
        outs[owner][:, WIDTH:] = sent[owner * local_rows : (owner + 1) * local_rows].astype(outs[owner].dtype)


def merge_kernel(*refs):
    parts, out = refs[:-1], refs[-1]
    levels = []
    for part in parts:
        terms = part[:, WIDTH:].astype(jnp.float32)
        levels.append(terms + pltpu.roll(terms, LANES - STRIDE, 1) + pltpu.roll(terms, LANES - 2 * STRIDE, 1))
    top = functools.reduce(jnp.maximum, levels)
    shares = [jnp.exp2(level - top) for level in levels]
    whole = 1.0 / functools.reduce(jnp.add, shares)
    shares = [share * whole for share in shares]
    for head in range(QUERY_HEADS):
        total = functools.reduce(
            jnp.add,
            [
                share[:, head : head + 1] * part[:, HEADS[head]].astype(jnp.float32)
                for share, part in zip(shares, parts)
            ],
        )
        out[:, HEADS[head]] = total.astype(out.dtype)


def held(memory, arrays):
    return [pltpu.with_memory_space_constraint(x, memory) for x in arrays]


def swap(x, offset):
    return lax.ppermute(x, "rows", [(i, i ^ offset) for i in range(lax.axis_size("rows"))])


def by_head(x):
    return jnp.transpose(x.reshape(-1, KV_HEADS, HEAD_DIM), (1, 0, 2)).reshape(-1, HEAD_DIM)


def after(x, *earlier):
    return lax.optimization_barrier((x, *earlier))


def shards(queries, prefix_keys, prefix_values, tree_keys, tree_values, parents):
    size = lax.axis_size("rows")
    bits = size.bit_length() - 1
    near_bits = (bits + 1) // 2
    near = 2**near_bits
    far = size // near
    local_rows = queries.shape[0]
    slab, row_width = prefix_keys.shape
    far_offsets = [0] + [near * i | 1 for i in range(1, far)]
    far_order = far_offsets[2:] + far_offsets[1:2]
    vmem = pl.BlockSpec(memory_space=pltpu.VMEM)
    hbm = pl.BlockSpec(memory_space=pltpu.HBM)
    params = pltpu.CompilerParams(vmem_limit_bytes=16 * 2**20)
    own_rest = pl.pallas_call(
        rest_kernel,
        out_shape=pltpu.VMEM((slab + 2 * local_rows, row_width), prefix_values.dtype),
        in_specs=[hbm] * 3,
        out_specs=vmem,
        scratch_shapes=[
            pltpu.VMEM((2, KV_HEADS * local_rows, HEAD_DIM), tree_keys.dtype),
            pltpu.SemaphoreType.DMA((2 + CHUNKS,)),
        ],
        compiler_params=params,
    )(*held(pltpu.HBM, [prefix_values, by_head(tree_keys), by_head(tree_values)]))

    owner_offsets = [0] + far_order
    key_pieces, rest_pieces = {0: prefix_keys}, {0: own_rest}
    for bit in reversed(range(1, near_bits)):
        for offset in list(key_pieces):
            step = 1 << bit
            key_pieces[offset ^ step] = swap(key_pieces[offset], step)
            rest_pieces[offset ^ step] = swap(rest_pieces[offset], step)
    block_offsets = list(key_pieces)
    sibling_offsets = [offset ^ 1 for offset in block_offsets]
    last_offset = list(rest_pieces)[-1]
    parents, rest_pieces[last_offset] = after(parents, rest_pieces[last_offset])
    mask = pl.pallas_call(
        functools.partial(mask_kernel, owner_offsets, block_offsets + sibling_offsets, local_rows),
        out_shape=pltpu.VMEM((far * local_rows, near * (slab + 2 * local_rows)), jnp.float32),
        in_specs=[vmem],
        out_specs=vmem,
        compiler_params=params,
    )(parents[None, :])
    all_queries = {0: queries}
    for offset in far_order:
        sent = queries
        if offset == far_order[-1]:
            sent, key_pieces[block_offsets[-1]] = after(sent, key_pieces[block_offsets[-1]])
        all_queries[offset] = swap(sent, offset)
    gathered = pl.pallas_call(
        rows_kernel,
        out_shape=pltpu.VMEM((far * local_rows, WIDTH), queries.dtype),
        in_specs=[vmem] * far,
        out_specs=vmem,
        compiler_params=params,
        cost_estimate=SCHEDULE_LAST,
    )(*held(pltpu.VMEM, [all_queries[offset] for offset in owner_offsets]))
    blocks = list(key_pieces.values()) + list(rest_pieces.values())[:-1]
    bundle = pl.pallas_call(
        stack_kernel,
        out_shape=pltpu.VMEM((sum(block.shape[0] for block in blocks), row_width), prefix_keys.dtype),
        in_specs=[vmem] * len(blocks),
        out_specs=vmem,
        compiler_params=params,
    )(*held(pltpu.VMEM, blocks))
    last_rest = list(rest_pieces.values())[-1]
    far_bundle, far_rest = swap(bundle, 1), swap(last_rest, 1)
    count = len(block_offsets)
    operands = [gathered, bundle, last_rest, far_bundle, far_rest, mask]
    partials = pl.pallas_call(
        functools.partial(attend_kernel, far, count, slab),
        out_shape=[
            pltpu.VMEM((local_rows, WIDTH + LANES), jnp.bfloat16 if offset else jnp.float32)
            for offset in owner_offsets
        ],
        in_specs=[vmem] * len(operands),
        out_specs=[vmem] * far,
        compiler_params=params,
    )(*held(pltpu.VMEM, operands))
    parts = [partials[0]]
    for offset in far_offsets[-1:] + far_offsets[1:-1]:
        parts.append(swap(partials[owner_offsets.index(offset)], offset))
    return pl.pallas_call(
        merge_kernel,
        out_shape=jax.ShapeDtypeStruct((local_rows, WIDTH), jnp.bfloat16),
        in_specs=[vmem] * far,
        out_specs=vmem,
        compiler_params=params,
    )(*held(pltpu.VMEM, parts))


def solution(mesh):
    placed = (
        P(("group", "rows"), None),
        P(("group", "rows"), None),
        P(("group", "rows"), None),
        P(("group", "rows"), None),
        P(("group", "rows"), None),
        P("group"),
    )
    return jax.shard_map(
        shards, mesh=mesh, in_specs=placed, out_specs=P(("group", "rows"), None), check_vma=False
    )
```
